256 devices in a mesh: ctx: 8 (over z_lo, y), dp: 32 (over x, z_hi, core).
Axes of the slice: x: 4, y: 4, z: 8 (z_hi: 4, z_lo: 2; z = z_hi * 2 + z_lo), core: 2. Of those that a mesh axis runs over, the one named last changes fastest.
Arguments:
- queries: bfloat16 [32, 1024, 2048], P('dp', 'ctx'), may hold values from -54 to 54
- key_states: bfloat16 [32, 1024, 1024], P('dp', 'ctx'), may hold values from -33 to 33
- value_states: bfloat16 [32, 1024, 1024], P('dp', 'ctx'), may hold values from -6 to 6
- saved_output: bfloat16 [32, 1024, 2048], P('dp', 'ctx'), may hold values from -6 to 6
- output_grad: bfloat16 [32, 1024, 2048], P('dp', 'ctx'), may hold values from -2.5 to 2.5
- layer_input: bfloat16 [32, 1024, 4608], P('dp', 'ctx'), may hold values from -6 to 6
- document_lengths: int32 [32, 8], P('dp'), may hold values from 1 to 512, 1024 in all within a row
Outputs:
- query_grad: bfloat16 [32, 1024, 2048], P('dp', 'ctx')
- key_grad: bfloat16 [32, 1024, 1024], P('dp', 'ctx')
- value_grad: bfloat16 [32, 1024, 1024], P('dp', 'ctx')
- weight_grad: float32 [4608, 1024], P('dp', 'ctx')
The draws below stay inside these ranges and needn't reach their ends.
Inputs may be any that keep to these rules, and one draw needn't show every extreme that they name: `document_lengths`: in every pack the 8 lengths sum to 1024 and the longest is exactly 512.
All inputs are finite; a program needn't handle non-finite values.
Results may differ from the reference program's by a relative error of at most 0.018.
Values may be sent and summed in bfloat16 or wider, within the bound.
No kernel may reach another device: no remote copies, remote signals or barrier semaphores. Data moves between devices by JAX's collectives and lax.ppermute only.
A program may use at most 128 MiB of HBM per device.

```python
import math
import jax
import jax.numpy as jnp
import numpy as np
from jax import lax

D = 4608
HQ = 16
KEY_VALUE_HEADS = 8
HEAD_SIZE = 128
DOCS = 8
ROWS = 128
QUERY_PER_KEY = 2
KVW = 1024
PACK_LENGTH = 1024
PACKS = 32
N_CTX = 8


def draw_queries(key, part):
    key = jax.random.fold_in(key, 11)
    first, second, third = jax.random.split(key, 3)
    shape = (PACKS, PACK_LENGTH, HQ * HEAD_SIZE)
    base = jnp.clip(jax.random.normal(first, shape, jnp.float32), -6.0, 6.0)
    row_matrix = jnp.exp(jax.random.uniform(second, (PACKS, PACK_LENGTH, 1), jnp.float32, math.log(0.3), math.log(3.0)))
    cols = jnp.exp(jax.random.uniform(third, (1, 1, HQ * HEAD_SIZE), jnp.float32, math.log(0.3), math.log(3.0)))
    return (base * row_matrix * cols).astype(jnp.bfloat16)


def draw_key_states(key, part):
    key = jax.random.fold_in(key, 23)
    first, second = jax.random.split(key, 2)
    shape = (PACKS, PACK_LENGTH, KVW)
    row_matrix = jnp.exp(jax.random.uniform(second, (PACKS, PACK_LENGTH, 1), jnp.float32, math.log(0.3), math.log(3.0)))
    base = jnp.clip(jax.random.normal(first, shape, jnp.float32), -6.0, 6.0)
    return (base * row_matrix).astype(jnp.bfloat16)


def strengthened(values, rng, source, target, parts, factor):
    def block_of(position):
        return (jnp.arange(values.shape[position]) // (values.shape[position] // parts)).reshape((-1,) + (1,) * (values.ndim - 1 - position))

    one_side = jax.random.permutation(rng, parts)[block_of(target)]
    other_side = (block_of(target) + parts // 2) % parts
    return jnp.where((block_of(source) == one_side) | (block_of(source) == other_side), factor * values, values)


def shard_levels(stream_key, dims, cuts, least, high):
    def one(axis_at, shards_of):
        heights = jax.random.uniform(jax.random.fold_in(jax.random.fold_in(stream_key, 6), axis_at), (shards_of,), jnp.float32, least / len(cuts), high / len(cuts))
        return jnp.repeat(jnp.exp(heights), dims[axis_at] // shards_of).reshape((-1,) + (1,) * (len(dims) - axis_at - 1))

    loudness = one(*cuts[0])
    for cut in cuts[1:]:
        loudness = loudness * one(*cut)
    return loudness


def length_profile(number_of, total, reach, skew):
    weights = [(1 << 20) // math.isqrt(standing ** skew) + 1 for standing in range(2, number_of + 1)]
    spare, given = total - reach - (number_of - 1), [1] * (number_of - 1)
    while spare > 0:
        free = [i for i in range(number_of - 1) if given[i] < reach]
        mass, left = sum([weights[i] for i in free]), spare
        for i in free:
            extra = min(reach - given[i], max(1, left * weights[i] // mass), spare)
            given[i] = given[i] + extra
            spare = spare - extra
    return np.array([reach] + given)


def ragged_sizes(key, count, total, limit, lean):
    if count == 2:
        one = jax.random.randint(key, (), max(1, total - limit), min(limit, total - 1) + 1)
        return jnp.stack([one, total - one])
    sizes = jnp.asarray(length_profile(count, total, limit, lean), jnp.int32)
    couples = (count - 1) // 2
    donor, receiver = sizes[1:1 + 2 * couples:2], sizes[2:2 + 2 * couples:2]
    room = jnp.minimum(donor - 1, limit - receiver)
    shifted = jax.random.randint(jax.random.fold_in(key, 1), (couples,), 0, 1 << 20) % (room + 1)
    sizes = sizes.at[1:1 + 2 * couples:2].set(donor - shifted).at[2:2 + 2 * couples:2].set(receiver + shifted)
    return sizes[jax.random.permutation(jax.random.fold_in(key, 2), count)]


def scatter_about(own_key, dims, deviation, bound, shards=(), held_as=jnp.bfloat16):
    values = deviation * jax.random.normal(own_key, dims, jnp.float32)
    if shards:
        values = values * shard_levels(own_key, dims, shards, -0.22, 0.18)
    return jnp.clip(values, -bound, bound).astype(held_as)


def bell_draw_with(key, dims, width, reach, shards, heavy, kind=jnp.bfloat16):
    result = width * jax.random.normal(key, dims, jnp.float32)
    if shards:
        result = result * shard_levels(key, dims, shards, -0.22, 0.18)
    return jnp.clip(strengthened(result, jax.random.fold_in(key, 3), *heavy), -reach, reach).astype(kind)


def setup_inputs(seed: int = 0) -> dict:
    keys = jax.random.split(jax.random.key(seed), 8)
    queries = draw_queries(jax.random.fold_in(keys[7], 71), 0)
    key_states = draw_key_states(jax.random.fold_in(keys[7], 71), 0)
    value_states = scatter_about(keys[2], (PACKS, PACK_LENGTH, KVW), 1.0, 6.0, ((0, 32), (1, 8)))
    saved_output = scatter_about(keys[3], (PACKS, PACK_LENGTH, HQ * HEAD_SIZE), 1.0, 6.0, ((0, 32), (1, 8)))
    output_grad = scatter_about(keys[4], (PACKS, PACK_LENGTH, HQ * HEAD_SIZE), 0.25, 2.5, ((0, 32), (1, 8)))
    layer_input = bell_draw_with(keys[5], (PACKS, PACK_LENGTH, D), 1.0, 6.0, ((0, 32), (1, 8)), (0, 2, 32, 2.75))
    document_lengths = jax.vmap(lambda own: ragged_sizes(own, DOCS, PACK_LENGTH, PACK_LENGTH // 2, 2))(jax.random.split(keys[6], PACKS)).reshape((PACKS, DOCS)).astype(jnp.int32)
    return dict(queries=queries, key_states=key_states, value_states=value_states, saved_output=saved_output, output_grad=output_grad, layer_input=layer_input, document_lengths=document_lengths)


CAP = 50.0
SCALE = 144.0 ** (-0.5)

def doc_ids(lengths, positions):
    ends = jnp.cumsum(lengths)
    return lax.optimization_barrier(jnp.sum((positions[:, None] >= ends[None, :]).astype(jnp.int32), axis=1))

def pack_grads(queries, key_matrix, value_matrix, output_matrix, gradient_list, inputs, lengths):
    positions = jnp.arange(PACK_LENGTH, dtype=jnp.int32)
    ident = doc_ids(lengths, positions)
    live = (ident[:, None] == ident[None, :]) & (positions[None, :] <= positions[:, None])
    live = live[None, None]
    query_head_view = queries.astype(jnp.float32).reshape(PACK_LENGTH, KEY_VALUE_HEADS, QUERY_PER_KEY, HEAD_SIZE)
    key_head_view = key_matrix.astype(jnp.float32).reshape(PACK_LENGTH, KEY_VALUE_HEADS, HEAD_SIZE)
    value_head_view = value_matrix.astype(jnp.float32).reshape(PACK_LENGTH, KEY_VALUE_HEADS, HEAD_SIZE)
    output_head_view = output_matrix.astype(jnp.float32).reshape(PACK_LENGTH, KEY_VALUE_HEADS, QUERY_PER_KEY, HEAD_SIZE)
    grad_head_view = gradient_list.astype(jnp.float32).reshape(PACK_LENGTH, KEY_VALUE_HEADS, QUERY_PER_KEY, HEAD_SIZE)
    raw = jnp.einsum('qgrd,kgd->grqk', query_head_view, key_head_view) * SCALE
    capped_logits = CAP * jnp.tanh(raw / CAP)
    total = lax.optimization_barrier(jnp.sum(jnp.where(live, jnp.exp(capped_logits), 0.0), axis=-1))
    lse = jnp.log(total)
    prob = jnp.where(live, jnp.exp(capped_logits - lse[..., None]), 0.0)
    delta = jnp.einsum('qgrd,qgrd->grq', grad_head_view, output_head_view)
    dprob = jnp.einsum('qgrd,kgd->grqk', grad_head_view, value_head_view)
    dscore = (prob * (dprob - delta[..., None]) * (1.0 - (capped_logits / CAP) ** 2) * SCALE).astype(jnp.bfloat16)
    prob_low = prob.astype(jnp.bfloat16)
    dscore_wide = dscore.astype(jnp.float32)
    query_grad = jnp.einsum('grqk,kgd->qgrd', dscore_wide, key_head_view).reshape(PACK_LENGTH, HQ * HEAD_SIZE).astype(jnp.bfloat16)
    key_grad = jnp.einsum('grqk,qgrd->kgd', dscore_wide, query_head_view).reshape(PACK_LENGTH, KVW).astype(jnp.bfloat16)
    value_grad = jnp.einsum('grqk,qgrd->kgd', prob_low.astype(jnp.float32), grad_head_view).reshape(PACK_LENGTH, KVW).astype(jnp.bfloat16)
    factor = 1.0 / math.sqrt(float(PACKS * PACK_LENGTH))
    blocks_in = inputs.astype(jnp.float32).reshape(N_CTX, ROWS, D)
    blocks_val = value_grad.astype(jnp.float32).reshape(N_CTX, ROWS, KVW)

    def block_term(carry, pair):
        term = jnp.dot(pair[0].T, pair[1], preferred_element_type=jnp.float32) * factor
        rounded = lax.optimization_barrier(term.astype(jnp.bfloat16))
        return (carry + rounded.astype(jnp.float32), None)
    summed, _ = lax.scan(block_term, jnp.zeros((D, KVW), jnp.float32), (blocks_in, blocks_val))
    return (summed, query_grad, key_grad, value_grad)

def reference(queries, key_states, value_states, saved_output, output_grad, layer_input, document_lengths):

    def one_pack(carry, packed):
        summed, query_grad, key_grad, value_grad = pack_grads(*packed)
        return (carry + summed, (query_grad, key_grad, value_grad))
    weight_grad, (query_grad, key_grad, value_grad) = lax.scan(one_pack, jnp.zeros((D, KVW), jnp.float32), (queries, key_states, value_states, saved_output, output_grad, layer_input, document_lengths))
    return (query_grad, key_grad, value_grad, weight_grad)
```

```python
import math

import jax
import jax.numpy as jnp
from jax import lax
from jax.experimental import pallas as pl
from jax.experimental.pallas import tpu as pltpu
from jax.sharding import PartitionSpec as P

ROWS = 128
HEAD = 128
BLOCKS = 8
TAIL = 16
PACKED = 768
BACK = 512
CAP = 50.0
SCALE = 144.0 ** (-0.5)
BF = jnp.bfloat16
F32 = jnp.float32
OFFSETS = [(a, b) for a in range(2) for b in range(4)]
VMEM_LIMIT = 48 * 1024 * 1024


def spread(block, place):
    route = []
    for ctx in range(8):
        for dp in range(32):
            here = (dp // 8, ctx % 4, (dp // 2) % 4 * 2 + ctx // 4, dp % 2)
            x, y, z, core = place(*here)
            x, y, z = x % 4, y % 4, z % 8
            route.append((ctx * 32 + dp, ((z % 2) * 4 + y) * 32 + x * 8 + z // 2 * 2 + core))
    return lax.ppermute(block, ("ctx", "dp"), route)


def nt(left, right):
    return lax.dot_general(left, right, (((1,), (1,)), ((), ())), preferred_element_type=F32)


def nn(left, right):
    return lax.dot_general(left, right, (((1,), (0,)), ((), ())), preferred_element_type=F32)


def partner(mine, a, b, sign):
    return ((mine // 4) ^ a) * 4 + (mine + sign * b) % 4


def split_three(value):
    first = value.astype(BF)
    rest = value - first.astype(F32)
    second = rest.astype(BF)
    third = (rest - second.astype(F32)).astype(BF)
    return first, second, third


def pack_kernel(where, q, k, v, do, o, *outs):
    mine = where[0]
    product = do[...].astype(F32) * o[...].astype(F32)
    high = product.astype(BF)
    low = (product - high.astype(F32)).astype(BF)
    row = lax.broadcasted_iota(jnp.int32, (TAIL, 2048), 0)
    col = lax.broadcasted_iota(jnp.int32, (TAIL, 2048), 1)
    pick = (row == col // HEAD).astype(BF)
    delta = nt(pick, high) + nt(pick, low)
    first, second, third = split_three(delta)
    for (a, b), out in zip(OFFSETS, outs):
        target = partner(mine, a, b, 1)
        wide = pl.ds(pl.multiple_of(target * 256, 256), 256)
        thin = pl.ds(pl.multiple_of(target * 128, 128), 128)
        out[0:ROWS, 0:256] = q[:, wide]
        out[0:ROWS, 256:512] = do[:, wide]
        out[0:ROWS, 512:640] = k[:, thin]
        out[0:ROWS, 640:768] = v[:, thin]
        out[ROWS:, 0:128] = first
        out[ROWS:, 128:256] = second
        out[ROWS:, 256:384] = third
        out[ROWS:, 384:768] = jnp.zeros((TAIL, 384), BF)


def attention_kernel(where, lengths, *refs):
    pieces = refs[:8]
    backs = refs[8:16]
    values_a, values_b = refs[16:18]
    held, key_turned, dq, dk, dv, sems = refs[18:]
    mine = where[0]
    core = where[1]
    copies = []
    for n, ((a, b), piece) in enumerate(zip(OFFSETS, pieces)):
        copy = pltpu.make_async_copy(piece, held.at[partner(mine, a, b, -1)], sems.at[n])
        copy.start()
        copies.append(copy)
    dk[...] = jnp.zeros_like(dk)
    dv[...] = jnp.zeros_like(dv)
    ends = []
    total = 0
    for d in range(8):
        total = total + lengths[0, d]
        ends.append(total)
    for copy in copies:
        copy.wait()
    for n in range(BLOCKS):
        key_turned[n] = held[n, 0:ROWS, 512:640].T

    def block(b, carry):
        base = b * ROWS
        first = 0
        for end in ends:
            first = jnp.where(base >= end, end, first)
        kb0 = first // ROWS
        count = b - kb0 + 1
        lane = lax.broadcasted_iota(jnp.int32, (1, 256), 1)
        query = base + lane % ROWS
        begin = jnp.zeros((1, 256), jnp.int32)
        for end in ends:
            begin = jnp.where(query >= end, end, begin)
        tail = held[b, ROWS:, 0:384].astype(F32)
        tail = tail[:, 0:128] + tail[:, 128:256] + tail[:, 256:384]
        head = lax.broadcasted_iota(jnp.int32, (TAIL, 128), 0)
        delta = jnp.concatenate(
            [
                jnp.sum(jnp.where(head == 2 * mine + s, tail, 0.0), axis=0, keepdims=True)
                for s in range(2)
            ],
            axis=1,
        )
        queries = jnp.concatenate([held[b, 0:ROWS, 0:128], held[b, 0:ROWS, 128:256]], axis=0)
        grads = jnp.concatenate([held[b, 0:ROWS, 256:384], held[b, 0:ROWS, 384:512]], axis=0)
        sub = lax.broadcasted_iota(jnp.int32, (ROWS, 256), 0)

        def window(number):
            powers, tanhs = [], []
            sums = jnp.zeros((1, 256), F32)
            for n in range(number):
                kb = kb0 + n
                raw = nt(held[kb, 0:ROWS, 512:640], queries)
                tanh = jnp.tanh(raw * (SCALE / CAP))
                key = sub + kb * ROWS
                live = key >= begin
                if n == number - 1:
                    live = live & (key <= query)
                power = jnp.where(live, jnp.exp(CAP * tanh), 0.0)
                sums = sums + jnp.sum(power, axis=0, keepdims=True)
                powers.append(power)
                tanhs.append(tanh)
            inverse = 1.0 / sums
            turned = jnp.zeros((HEAD, 256), F32)
            for n in range(number):
                kb = kb0 + n
                prob = powers[n] * inverse
                dprob = nt(held[kb, 0:ROWS, 640:768], grads)
                slope = SCALE - (SCALE * tanhs[n]) * tanhs[n]
                dscore = (prob * (dprob - delta) * slope).astype(BF)
                dv[kb] += nn(prob.astype(BF), grads)
                dk[kb] += nn(dscore, queries)
                turned = turned + nn(key_turned[kb], dscore)
            straight = turned.T
            dq[b, :, 0:128] = straight[0:ROWS].astype(BF)
            dq[b, :, 128:256] = straight[ROWS:].astype(BF)

        for number in range(1, 6):

            @pl.when(count == number)
            def _():
                window(number)

        return carry

    lax.fori_loop(0, BLOCKS, block, 0)
    for (a, b), back in zip(OFFSETS, backs):
        target = partner(mine, a, b, 1)
        back[:, 0:256] = dq[target]
        back[:, 256:384] = dk[target].astype(BF)
        back[:, 384:512] = dv[target].astype(BF)
    for n in range(4):
        values_a[n * ROWS : (n + 1) * ROWS, :] = dv[core * 4 + n].astype(BF)
        values_b[n * ROWS : (n + 1) * ROWS, :] = dv[(1 - core) * 4 + n].astype(BF)


def turn_kernel(where, *refs):
    pieces, out = refs[:8], refs[8]
    held, sems = refs[9:]
    mine, core = where[0], where[1]
    copies = []
    for n in range(8):
        pack = core if n < 4 else 1 - core
        slot = pack * 4 + (mine - n % 4) % 4
        copy = pltpu.make_async_copy(pieces[n], held.at[slot], sems.at[n])
        copy.start()
        copies.append(copy)
    for copy in copies:
        copy.wait()

    @pl.loop(0, 8)
    def _(n):
        out[n] = held[n].T


def weight_kernel(where, turned, *refs):
    pieces = refs[:8]
    outs = refs[8:12]
    left, right, sems = refs[12:]
    mine, core, x = where[0], where[1], where[2]
    half = mine // 4
    copies = []
    for n in range(8):
        copy = pltpu.make_async_copy(
            turned.at[n], left.at[:, pl.ds(n * ROWS, ROWS)], sems.at[8 + n]
        )
        copy.start()
        copies.append(copy)
    for n in range(8):
        pack = half if n < 4 else 1 - half
        source = (mine - n % 4) % 4
        copy = pltpu.make_async_copy(
            pieces[n],
            right.at[
                pl.ds(pl.multiple_of(pack * 512, 512), 512),
                pl.ds(pl.multiple_of(source * 128, 128), 128),
            ],
            sems.at[n],
        )
        copy.start()
        copies.append(copy)
    for copy in copies:
        copy.wait()
    factor = 1.0 / math.sqrt(32768.0)
    for step, out in enumerate(outs):
        target = (x + step) % 4
        rows = left[pl.ds(pl.multiple_of(target * 288, 32), 288), :]
        out[...] = (nn(rows, right[...]) * factor).astype(BF)


def sum_kernel(where, first, second, third, fourth, *outs):
    z = where[3]
    total = first[...].astype(F32) + second[...].astype(F32)
    total = total + third[...].astype(F32) + fourth[...].astype(F32)
    total = total.astype(BF)
    blocks = [
        total[u * 144 : (u + 1) * 144, w * 128 : (w + 1) * 128] for w in range(4) for u in range(2)
    ]
    for m, value in enumerate(blocks):
        for step, out in enumerate(outs):

            @pl.when((z ^ step) == m)
            def _():
                out[...] = value


def last_kernel(*refs):
    total = refs[0][...].astype(F32)
    for ref in refs[1:8]:
        total = total + ref[...].astype(F32)
    refs[8][...] = total


def unpack_kernel(where, *refs):
    pieces = refs[:8]
    query_grad, key_grad, value_grad = refs[8:]
    mine = where[0]
    for (a, b), piece in zip(OFFSETS, pieces):
        source = partner(mine, a, b, -1)
        wide = pl.ds(pl.multiple_of(source * 256, 256), 256)
        thin = pl.ds(pl.multiple_of(source * 128, 128), 128)
        query_grad[:, wide] = piece[:, 0:256]
        key_grad[:, thin] = piece[:, 256:384]
        value_grad[:, thin] = piece[:, 384:512]


SMEM = pl.BlockSpec(memory_space=pltpu.SMEM)
VMEM = pl.BlockSpec(memory_space=pltpu.VMEM)
ANY = pl.BlockSpec(memory_space=pl.ANY)


def shape(*dims, dtype=BF):
    return jax.ShapeDtypeStruct(dims, dtype)


def call(kernel, outs, ins, scratch=(), flops=0, moved=0):
    return pl.pallas_call(
        kernel,
        out_shape=outs,
        in_specs=ins,
        out_specs=jax.tree.map(lambda _: VMEM, outs),
        scratch_shapes=list(scratch),
        compiler_params=pltpu.CompilerParams(vmem_limit_bytes=VMEM_LIMIT),
        cost_estimate=pl.CostEstimate(flops=flops, bytes_accessed=moved, transcendentals=0),
    )


def body(
    queries, key_states, value_states, saved_output, output_grad, layer_input, document_lengths
):
    mine = lax.axis_index("ctx")
    dp = lax.axis_index("dp")
    core = dp % 2
    where = jnp.stack([mine, core, dp // 8, dp // 2 % 4 * 2 + mine // 4]).astype(jnp.int32)

    packed = call(pack_kernel, [shape(ROWS + TAIL, PACKED)] * 8, [SMEM] + [VMEM] * 5)(
        where, queries[0], key_states[0], value_states[0], output_grad[0], saved_output[0]
    )
    arrived = [packed[0]]
    for (a, b), block in list(zip(OFFSETS, packed))[1:]:
        arrived.append(spread(block, lambda x, y, z, c: (x, y + b, z ^ a, c)))

    inputs = layer_input[0]
    y = mine % 4
    own = []
    for b in range(4):
        piece = lax.dynamic_slice(inputs, (0, (y + b) % 4 * 1152), (ROWS, 1152))
        own.append(spread(piece, lambda x, y, z, c: (x, y + b, z, c)) if b else piece)
    other = [spread(piece, lambda x, y, z, c: (x, y, z, 1 - c)) for piece in own]
    turned = call(
        turn_kernel,
        shape(8, 1152, ROWS),
        [SMEM] + [ANY] * 8,
        [pltpu.VMEM((8, ROWS, 1152), BF), pltpu.SemaphoreType.DMA((8,))],
    )(where, *own, *other)

    results = call(
        attention_kernel,
        [shape(ROWS, BACK)] * 8 + [shape(512, HEAD)] * 2,
        [SMEM, SMEM] + [ANY] * 8,
        [
            pltpu.VMEM((BLOCKS, ROWS + TAIL, PACKED), BF),
            pltpu.VMEM((BLOCKS, HEAD, ROWS), BF),
            pltpu.VMEM((BLOCKS, ROWS, 256), BF),
            pltpu.VMEM((BLOCKS, ROWS, HEAD), F32),
            pltpu.VMEM((BLOCKS, ROWS, HEAD), F32),
            pltpu.SemaphoreType.DMA((8,)),
        ],
        flops=4_000_000_000,
        moved=4_000_000,
    )(where, document_lengths, *arrived)
    backs, values_a, values_b = results[:8], results[8], results[9]

    gathered = []
    for b in range(4):
        gathered.append(
            spread(values_a, lambda x, y, z, c: (x, y + b, z // 2 * 2 + c, z % 2))
        )
    for b in range(4):
        gathered.append(
            spread(values_b, lambda x, y, z, c: (x, y + b, z // 2 * 2 + 1 - c, z % 2))
        )

    parts = call(
        weight_kernel,
        [shape(288, 512)] * 4,
        [SMEM, ANY] + [ANY] * 8,
        [
            pltpu.VMEM((1152, 1024), BF),
            pltpu.VMEM((1024, 512), BF),
            pltpu.SemaphoreType.DMA((16,)),
        ],
        flops=1_300_000_000,
        moved=4_000_000,
    )(where, turned, *gathered)
    reduced = [parts[0]]
    for step in range(1, 4):
        reduced.append(spread(parts[step], lambda x, y, z, c: (x + step, y, z, c)))
    blocks = call(sum_kernel, [shape(144, 128)] * 8, [SMEM] + [VMEM] * 4)(where, *reduced)
    landed = []
    for step in range(8):
        landed.append(
            spread(
                blocks[step],
                lambda x, y, z, c: (y, (z ^ step) // 2, 2 * x + c, (z ^ step) % 2),
            )
        )
    weight_grad = call(last_kernel, shape(144, 128, dtype=F32), [VMEM] * 8)(*landed)

    returned = [backs[0]]
    for (a, b), block in list(zip(OFFSETS, backs))[1:]:
        returned.append(spread(block, lambda x, y, z, c: (x, y + b, z ^ a, c)))
    query_grad, key_grad, value_grad = call(
        unpack_kernel,
        [shape(ROWS, 2048), shape(ROWS, 1024), shape(ROWS, 1024)],
        [SMEM] + [VMEM] * 8,
    )(where, *returned)
    return query_grad[None], key_grad[None], value_grad[None], weight_grad


def solution(mesh):
    return jax.shard_map(
        body,
        mesh=mesh,
        in_specs=(P("dp", "ctx", None),) * 6 + (P("dp", None),),
        out_specs=(P("dp", "ctx", None),) * 3 + (P("dp", "ctx"),),
        check_vma=False,
    )
```

```python
import math

import jax
import jax.numpy as jnp
from jax import lax
from jax.experimental import pallas as pl
from jax.experimental.pallas import tpu as pltpu
from jax.sharding import PartitionSpec as P

ROWS = 128
HEAD = 128
BLOCKS = 8
TAIL = 16
PACKED = 768
BACK = 384
CAP = 50.0
SCALE = 144.0 ** (-0.5)
BF = jnp.bfloat16
F32 = jnp.float32
MIB = 1024 * 1024


def spread(block, place):
    route = []
    for ctx in range(8):
        for dp in range(32):
            here = (dp // 8, ctx % 4, (dp // 2) % 4 * 2 + ctx // 4, dp % 2)
            x, y, z, core = place(*here)
            x, y, z = x % 4, y % 4, z % 8
            route.append((ctx * 32 + dp, ((z % 2) * 4 + y) * 32 + x * 8 + z // 2 * 2 + core))
    return lax.ppermute(block, ("ctx", "dp"), route)


def over_ctx(block, k):
    return spread(block, lambda x, y, z, c: (x, y ^ k % 4, z ^ k // 4, c)) if k else block


def over_x(block, k):
    return spread(block, lambda x, y, z, c: (x ^ k, y, z, c)) if k else block


def over_y(block, k):
    return over_ctx(block, k)


def over_z(block, k):
    return spread(block, lambda x, y, z, c: (x, y, z ^ 2 * k, c)) if k else block


def over_core(block):
    return spread(block, lambda x, y, z, c: (x, y, z, 1 - c))


def after(value, *others):
    return lax.optimization_barrier((value, *others))[0]


def nt(left, right):
    return lax.dot_general(left, right, (((1,), (1,)), ((), ())), preferred_element_type=F32)


def nn(left, right):
    return lax.dot_general(left, right, (((1,), (0,)), ((), ())), preferred_element_type=F32)


def split_three(value):
    first = value.astype(BF)
    rest = value - first.astype(F32)
    second = rest.astype(BF)
    third = (rest - second.astype(F32)).astype(BF)
    return first, second, third


def pack_kernel(*refs):
    out = refs[5]
    q, k, v, do, o = refs[6:11]
    sems = refs[11]
    copies = []
    for n, (source, held) in enumerate(zip(refs[:5], refs[6:11])):
        copy = pltpu.make_async_copy(source, held, sems.at[n])
        copy.start()
        copies.append(copy)
    for copy in copies:
        copy.wait()
    product = do[...].astype(F32) * o[...].astype(F32)
    high = product.astype(BF)
    low = (product - high.astype(F32)).astype(BF)
    row = lax.broadcasted_iota(jnp.int32, (TAIL, 2048), 0)
    col = lax.broadcasted_iota(jnp.int32, (TAIL, 2048), 1)
    pick = (row == col // HEAD).astype(BF)
    delta = nt(pick, high) + nt(pick, low)
    first, second, third = split_three(delta)
    for n in range(BLOCKS):
        out[n, 0:ROWS, 0:256] = q[:, n * 256 : (n + 1) * 256]
        out[n, 0:ROWS, 256:512] = do[:, n * 256 : (n + 1) * 256]
        out[n, 0:ROWS, 512:640] = k[:, n * 128 : (n + 1) * 128]
        out[n, 0:ROWS, 640:768] = v[:, n * 128 : (n + 1) * 128]
        out[n, ROWS:, 0:128] = first
        out[n, ROWS:, 128:256] = second
        out[n, ROWS:, 256:384] = third
        out[n, ROWS:, 384:768] = jnp.zeros((TAIL, 384), BF)


def attention_kernel(where, lengths, *refs):
    packed, back = refs[:2]
    values = refs[2:6]
    held, key_turned, dk, dv, sem = refs[6:]
    mine = where[0]
    copy = pltpu.make_async_copy(packed, held, sem)
    copy.start()
    dk[...] = jnp.zeros_like(dk)
    dv[...] = jnp.zeros_like(dv)
    ends = []
    total = 0
    for d in range(8):
        total = total + lengths[0, d]
        ends.append(total)
    copy.wait()
    for n in range(BLOCKS):
        key_turned[n] = held[n, 0:ROWS, 512:640].T

    def block(b, carry):
        base = b * ROWS
        first = 0
        for end in ends:
            first = jnp.where(base >= end, end, first)
        kb0 = first // ROWS
        count = b - kb0 + 1
        lane = lax.broadcasted_iota(jnp.int32, (1, 256), 1)
        query = base + lane % ROWS
        begin = jnp.zeros((1, 256), jnp.int32)
        for end in ends:
            begin = jnp.where(query >= end, end, begin)
        tail = held[b, ROWS:, 0:384].astype(F32)
        tail = tail[:, 0:128] + tail[:, 128:256] + tail[:, 256:384]
        head = lax.broadcasted_iota(jnp.int32, (TAIL, 128), 0)
        delta = jnp.concatenate(
            [
                jnp.sum(jnp.where(head == 2 * mine + s, tail, 0.0), axis=0, keepdims=True)
                for s in range(2)
            ],
            axis=1,
        )
        queries = jnp.concatenate([held[b, 0:ROWS, 0:128], held[b, 0:ROWS, 128:256]], axis=0)
        grads = jnp.concatenate([held[b, 0:ROWS, 256:384], held[b, 0:ROWS, 384:512]], axis=0)
        sub = lax.broadcasted_iota(jnp.int32, (ROWS, 256), 0)

        def window(number):
            powers, tanhs = [], []
            sums = jnp.zeros((1, 256), F32)
            for n in range(number):
                kb = kb0 + n
                raw = nt(held[kb, 0:ROWS, 512:640], queries)
                tanh = jnp.tanh(raw * (SCALE / CAP))
                key = sub + kb * ROWS
                live = key >= begin
                if n == number - 1:
                    live = live & (key <= query)
                power = jnp.where(live, jnp.exp(CAP * tanh), 0.0)
                sums = sums + jnp.sum(power, axis=0, keepdims=True)
                powers.append(power)
                tanhs.append(tanh)
            inverse = 1.0 / sums
            turned = jnp.zeros((HEAD, 256), F32)
            for n in range(number):
                kb = kb0 + n
                prob = powers[n] * inverse
                dprob = nt(held[kb, 0:ROWS, 640:768], grads)
                slope = SCALE - (SCALE * tanhs[n]) * tanhs[n]
                dscore = (prob * (dprob - delta) * slope).astype(BF)
                dv[kb] += nn(prob.astype(BF), grads)
                dk[kb] += nn(dscore, queries)
                turned = turned + nn(key_turned[kb], dscore)
            straight = turned.T
            back[b, :, 0:128] = straight[0:ROWS].astype(BF)
            back[b, :, 128:256] = straight[ROWS:].astype(BF)

        for number in range(1, 6):

            @pl.when(count == number)
            def _():
                window(number)

        return carry

    lax.fori_loop(0, BLOCKS, block, 0)
    for n in range(BLOCKS):
        back[n, :, 256:384] = dk[n].astype(BF)
    for k in range(4):
        for half in range(2):
            values[k][half] = dv[half * 4 + (mine % 4 ^ k)].astype(BF)


def turn_kernel(where, *refs):
    pieces, low, high, far = refs[:4], refs[4], refs[5], refs[6]
    held, turned, sems = refs[7:]
    core = where[1]
    copies = []
    for n in range(4):
        copy = pltpu.make_async_copy(pieces[n], held.at[n], sems.at[n])
        copy.start()
        copies.append(copy)
    for copy in copies:
        copy.wait()

    for n in range(4):
        turned[...] = held[n].T
        lanes = slice(n * ROWS, (n + 1) * ROWS)
        for z in range(4):
            rows = pl.ds(z * 144, 144)
            near = (low, high)[z // 2]
            near[pl.ds(z % 2 * 144, 144), lanes] = turned[pl.ds(pl.multiple_of((z * 2 + core) * 144, 16), 144)]
            far[rows, lanes] = turned[pl.ds(pl.multiple_of((z * 2 + 1 - core) * 144, 16), 144)]


def join_kernel(where, *refs):
    pieces, joined, near, far = refs[:4], refs[4], refs[5], refs[6]
    mine = where[0]
    half = mine // 4
    for k, piece in enumerate(pieces):
        columns = pl.ds(pl.multiple_of((mine % 4 ^ k) * HEAD, HEAD), HEAD)
        joined[0, :, columns] = piece[0]
        joined[1, :, columns] = piece[1]
    near[...] = joined[half]
    far[...] = joined[1 - half]


def weight_kernel(where, *refs):
    lefts, rights, outs = refs[:6], refs[6:14], refs[14:18]
    left, right, total, sems = refs[18:]
    mine = where[0]
    half = mine // 4
    copies = [[], [], [], []]

    def fetch(n, source, target):
        copy = pltpu.make_async_copy(source, target, sems.at[n, len(copies[n])])
        copy.start()
        copies[n].append(copy)

    for n in range(4):
        if n % 2:
            fetch(n, lefts[2 + n // 2 * 3], left.at[n])
        else:
            fetch(n, lefts[n // 2 * 3], left.at[n, pl.ds(0, 288)])
            fetch(n, lefts[n // 2 * 3 + 1], left.at[n, pl.ds(288, 288)])
        for k in range(4):
            fetch(
                n,
                rights[n % 2 * 4 + k].at[half if n < 2 else 1 - half],
                right.at[n, pl.ds(k * ROWS, ROWS)],
            )
    value = jnp.zeros((576, 512), F32)
    for n in range(4):
        for copy in copies[n]:
            copy.wait()
        value = value + nn(left[n], right[n])
    total[...] = (value * (1.0 / math.sqrt(32768.0))).astype(BF)
    for k, out in enumerate(outs):
        out[...] = total[:, pl.ds(pl.multiple_of((mine % 4 ^ k) * HEAD, HEAD), HEAD)]


def sum_kernel(where, *refs):
    total = refs[8]
    z_hi = where[2]
    value = refs[0][...].astype(F32)
    for ref in refs[1:4]:
        value = value + ref[...].astype(F32)
    total[...] = value.astype(BF)
    for k, out in enumerate(refs[4:8]):
        out[...] = total[pl.ds(pl.multiple_of((z_hi ^ k) * 144, 16), 144)]


def last_kernel(*refs):
    total = refs[0][...].astype(F32)
    for ref in refs[1:4]:
        total = total + ref[...].astype(F32)
    refs[4][...] = total


def unpack_kernel(where, returned, near, far, query_grad, key_grad, value_grad):
    half = where[0] // 4
    for n in range(BLOCKS):
        query_grad[:, n * 256 : (n + 1) * 256] = returned[n, :, 0:256]
        key_grad[:, n * 128 : (n + 1) * 128] = returned[n, :, 256:384]
    value_grad[:, pl.ds(pl.multiple_of(half * 512, 512), 512)] = near[...]
    value_grad[:, pl.ds(pl.multiple_of((1 - half) * 512, 512), 512)] = far[...]


SMEM = pl.BlockSpec(memory_space=pltpu.SMEM)
VMEM = pl.BlockSpec(memory_space=pltpu.VMEM)
ANY = pl.BlockSpec(memory_space=pl.ANY)


def shape(*dims, dtype=BF):
    return jax.ShapeDtypeStruct(dims, dtype)


def call(kernel, outs, ins, scratch=(), flops=0, moved=0, limit=16):
    return pl.pallas_call(
        kernel,
        out_shape=outs,
        in_specs=ins,
        out_specs=jax.tree.map(lambda _: VMEM, outs),
        scratch_shapes=list(scratch),
        compiler_params=pltpu.CompilerParams(vmem_limit_bytes=limit * MIB),
        cost_estimate=pl.CostEstimate(flops=flops, bytes_accessed=moved, transcendentals=0),
    )


def body(
    queries, key_states, value_states, saved_output, output_grad, layer_input, document_lengths
):
    mine = lax.axis_index("ctx")
    dp = lax.axis_index("dp")
    x = dp // 8
    where = jnp.stack([mine, dp % 2, dp // 2 % 4]).astype(jnp.int32)

    packed = call(
        pack_kernel,
        shape(BLOCKS, ROWS + TAIL, PACKED),
        [ANY] * 5,
        [
            pltpu.VMEM((ROWS, 2048), BF),
            pltpu.VMEM((ROWS, 1024), BF),
            pltpu.VMEM((ROWS, 1024), BF),
            pltpu.VMEM((ROWS, 2048), BF),
            pltpu.VMEM((ROWS, 2048), BF),
            pltpu.SemaphoreType.DMA((5,)),
        ],
        limit=60,
    )(queries[0], key_states[0], value_states[0], output_grad[0], saved_output[0])
    arrived = lax.all_to_all(packed, "ctx", 0, 0, tiled=True)

    inputs = layer_input[0]
    own = []
    for k in range(4):
        piece = lax.dynamic_slice(inputs, (0, (x ^ k) * 1152), (ROWS, 1152))
        own.append(over_x(after(piece, packed), k))
    near_low, near_high, far_rows = call(
        turn_kernel,
        [shape(288, 512)] * 2 + [shape(576, 512)],
        [SMEM] + [ANY] * 4,
        [
            pltpu.VMEM((4, ROWS, 1152), BF),
            pltpu.VMEM((1152, ROWS), BF),
            pltpu.SemaphoreType.DMA((4,)),
        ],
    )(where, *own)
    far_rows = over_core(far_rows)
    across_low = over_ctx(near_low, 4)

    back, *values = call(
        attention_kernel,
        [shape(BLOCKS, ROWS, BACK)] + [shape(2, ROWS, HEAD)] * 4,
        [SMEM, SMEM, ANY],
        [
            pltpu.VMEM((BLOCKS, ROWS + TAIL, PACKED), BF),
            pltpu.VMEM((BLOCKS, HEAD, ROWS), BF),
            pltpu.VMEM((BLOCKS, ROWS, HEAD), F32),
            pltpu.VMEM((BLOCKS, ROWS, HEAD), F32),
            pltpu.SemaphoreType.DMA,
        ],
        flops=4_000_000_000,
        moved=4_000_000,
    )(where, document_lengths, arrived)

    values = [after(value, across_low) for value in values]
    across_high = over_ctx(near_high, 4)
    across_far = over_ctx(far_rows, 4)
    pieces = [after(over_y(values[k], k), across_high) for k in range(4)]
    joined, near, far = call(
        join_kernel,
        [shape(2, ROWS, 512), shape(ROWS, 512), shape(ROWS, 512)],
        [SMEM] + [VMEM] * 4,
    )(where, *pieces)
    rights = [over_x(joined, k) for k in range(4)]
    rights = rights + [over_core(right) for right in rights]
    returned = lax.all_to_all(after(back, joined), "ctx", 0, 0, tiled=True)

    parts = call(
        weight_kernel,
        [shape(576, HEAD)] * 4,
        [SMEM] + [ANY] * 14,
        [
            pltpu.VMEM((4, 576, 512), BF),
            pltpu.VMEM((4, 512, 512), BF),
            pltpu.VMEM((576, 512), BF),
            pltpu.SemaphoreType.DMA((4, 6)),
        ],
        flops=1_300_000_000,
        moved=4_000_000,
    )(where, near_low, near_high, far_rows, across_low, across_high, across_far, *rights)
    far = over_ctx(far, 4)
    reduced = [over_y(parts[k], k) for k in range(4)]
    blocks = call(
        sum_kernel, [shape(144, HEAD)] * 4, [SMEM] + [VMEM] * 4, [pltpu.VMEM((576, HEAD), BF)]
    )(where, *reduced)
    landed = [over_z(blocks[k], k) for k in range(4)]
    weight_grad = call(last_kernel, shape(144, HEAD, dtype=F32), [VMEM] * 4)(*landed)
    query_grad, key_grad, value_grad = call(
        unpack_kernel,
        [shape(ROWS, 2048), shape(ROWS, 1024), shape(ROWS, 1024)],
        [SMEM] + [VMEM] * 3,
    )(where, returned, near, far)
    return query_grad[None], key_grad[None], value_grad[None], weight_grad


def solution(mesh):
    return jax.shard_map(
        body,
        mesh=mesh,
        in_specs=(P("dp", "ctx", None),) * 6 + (P("dp", None),),
        out_specs=(P("dp", "ctx", None),) * 3 + (P("dp", "ctx"),),
        check_vma=False,
    )
```

```python
import math

import jax
import jax.numpy as jnp
from jax import lax
from jax.experimental import pallas as pl
from jax.experimental.pallas import tpu as pltpu
from jax.sharding import PartitionSpec as P

ROWS = 128
HEAD = 128
BLOCKS = 8
TAIL = 16
PACKED = 768
BACK = 384
CAP = 50.0
SCALE = 144.0 ** (-0.5)
BF = jnp.bfloat16
F32 = jnp.float32
MIB = 1024 * 1024


def spread(block, place):
    route = []
    for ctx in range(8):
        for dp in range(32):
            here = (dp // 8, ctx % 4, (dp // 2) % 4 * 2 + ctx // 4, dp % 2)
            x, y, z, core = place(*here)
            x, y, z = x % 4, y % 4, z % 8
            route.append((ctx * 32 + dp, ((z % 2) * 4 + y) * 32 + x * 8 + z // 2 * 2 + core))
    return lax.ppermute(block, ("ctx", "dp"), route)


def over_ctx(block, k):
    return spread(block, lambda x, y, z, c: (x, y ^ k % 4, z ^ k // 4, c)) if k else block


def over_x(block, k):
    return spread(block, lambda x, y, z, c: (x ^ k, y, z, c)) if k else block


def over_y(block, k):
    return over_ctx(block, k)


def over_z(block, k):
    return spread(block, lambda x, y, z, c: (x, y, z ^ 2 * k, c)) if k else block


def over_core(block):
    return spread(block, lambda x, y, z, c: (x, y, z, 1 - c))


def after(value, *others):
    return lax.optimization_barrier((value, *others))[0]


def nt(left, right):
    return lax.dot_general(left, right, (((1,), (1,)), ((), ())), preferred_element_type=F32)


def nn(left, right):
    return lax.dot_general(left, right, (((1,), (0,)), ((), ())), preferred_element_type=F32)


def split_three(value):
    first = value.astype(BF)
    rest = value - first.astype(F32)
    second = rest.astype(BF)
    third = (rest - second.astype(F32)).astype(BF)
    return first, second, third


def pack_kernel(*refs):
    out = refs[5]
    q, k, v, do, o = refs[6:11]
    sems = refs[11]
    copies = []
    for n, (source, held) in enumerate(zip(refs[:5], refs[6:11])):
        copy = pltpu.make_async_copy(source, held, sems.at[n])
        copy.start()
        copies.append(copy)
    for copy in copies:
        copy.wait()
    product = do[...].astype(F32) * o[...].astype(F32)
    high = product.astype(BF)
    low = (product - high.astype(F32)).astype(BF)
    row = lax.broadcasted_iota(jnp.int32, (TAIL, 2048), 0)
    col = lax.broadcasted_iota(jnp.int32, (TAIL, 2048), 1)
    pick = (row == col // HEAD).astype(BF)
    delta = nt(pick, high) + nt(pick, low)
    first, second, third = split_three(delta)
    for n in range(BLOCKS):
        out[n, 0:ROWS, 0:256] = q[:, n * 256 : (n + 1) * 256]
        out[n, 0:ROWS, 256:512] = do[:, n * 256 : (n + 1) * 256]
        out[n, 0:ROWS, 512:640] = k[:, n * 128 : (n + 1) * 128]
        out[n, 0:ROWS, 640:768] = v[:, n * 128 : (n + 1) * 128]
        out[n, ROWS:, 0:128] = first
        out[n, ROWS:, 128:256] = second
        out[n, ROWS:, 256:384] = third
        out[n, ROWS:, 384:768] = jnp.zeros((TAIL, 384), BF)


def attention_kernel(where, lengths, *refs):
    held = refs[0]
    backs = refs[1:5]
    values = refs[5:9]
    key_turned, dq, dk, dv = refs[9:]
    mine = where[0]
    dk[...] = jnp.zeros_like(dk)
    dv[...] = jnp.zeros_like(dv)
    ends = []
    total = 0
    for d in range(8):
        total = total + lengths[0, d]
        ends.append(total)
    for n in range(BLOCKS):
        key_turned[n] = held[n, 0:ROWS, 512:640].T

    def block(b, carry):
        base = b * ROWS
        first = 0
        for end in ends:
            first = jnp.where(base >= end, end, first)
        kb0 = first // ROWS
        count = b - kb0 + 1
        lane = lax.broadcasted_iota(jnp.int32, (1, 256), 1)
        query = base + lane % ROWS
        begin = jnp.zeros((1, 256), jnp.int32)
        for end in ends:
            begin = jnp.where(query >= end, end, begin)
        tail = held[b, ROWS:, 0:384].astype(F32)
        tail = tail[:, 0:128] + tail[:, 128:256] + tail[:, 256:384]
        head = lax.broadcasted_iota(jnp.int32, (TAIL, 128), 0)
        delta = jnp.concatenate(
            [
                jnp.sum(jnp.where(head == 2 * mine + s, tail, 0.0), axis=0, keepdims=True)
                for s in range(2)
            ],
            axis=1,
        )
        queries = jnp.concatenate([held[b, 0:ROWS, 0:128], held[b, 0:ROWS, 128:256]], axis=0)
        grads = jnp.concatenate([held[b, 0:ROWS, 256:384], held[b, 0:ROWS, 384:512]], axis=0)
        sub = lax.broadcasted_iota(jnp.int32, (ROWS, 256), 0)

        def window(number):
            powers, tanhs = [], []
            sums = jnp.zeros((1, 256), F32)
            for n in range(number):
                kb = kb0 + n
                raw = nt(held[kb, 0:ROWS, 512:640], queries)
                tanh = jnp.tanh(raw * (SCALE / CAP))
                key = sub + kb * ROWS
                live = key >= begin
                if n == number - 1:
                    live = live & (key <= query)
                power = jnp.where(live, jnp.exp(CAP * tanh), 0.0)
                sums = sums + jnp.sum(power, axis=0, keepdims=True)
                powers.append(power)
                tanhs.append(tanh)
            inverse = 1.0 / sums
            turned = jnp.zeros((HEAD, 256), F32)
            for n in range(number):
                kb = kb0 + n
                prob = powers[n] * inverse
                dprob = nt(held[kb, 0:ROWS, 640:768], grads)
                slope = SCALE - (SCALE * tanhs[n]) * tanhs[n]
                dscore = (prob * (dprob - delta) * slope).astype(BF)
                dv[kb] += nn(prob.astype(BF), grads)
                dk[kb] += nn(dscore, queries)
                turned = turned + nn(key_turned[kb], dscore)
            straight = turned.T
            dq[b, :, 0:128] = straight[0:ROWS].astype(BF)
            dq[b, :, 128:256] = straight[ROWS:].astype(BF)

        for number in range(1, 6):

            @pl.when(count == number)
            def _():
                window(number)

        return carry

    lax.fori_loop(0, BLOCKS, block, 0)
    for k in range(4):
        for half in range(2):
            block = half * 4 + (mine % 4 ^ k)
            backs[k][half, :, 0:256] = dq[block]
            backs[k][half, :, 256:384] = dk[block].astype(BF)
            values[k][half] = dv[block].astype(BF)


def turn_kernel(where, *refs):
    pieces, near, far, turned = refs[:4], refs[4], refs[5], refs[6]
    core = where[1]
    for n in range(4):
        turned[...] = pieces[n][...].T
        lanes = slice(n * ROWS, (n + 1) * ROWS)
        for z in range(4):
            rows = pl.ds(z * 144, 144)
            near[rows, lanes] = turned[pl.ds(pl.multiple_of((z * 2 + core) * 144, 16), 144)]
            far[rows, lanes] = turned[pl.ds(pl.multiple_of((z * 2 + 1 - core) * 144, 16), 144)]


def join_kernel(where, *refs):
    pieces, joined, near, far = refs[:4], refs[4], refs[5], refs[6]
    mine = where[0]
    half = mine // 4
    for k, piece in enumerate(pieces):
        columns = pl.ds(pl.multiple_of((mine % 4 ^ k) * HEAD, HEAD), HEAD)
        joined[0, :, columns] = piece[0]
        joined[1, :, columns] = piece[1]
    near[...] = joined[half]
    far[...] = joined[1 - half]


def weight_kernel(where, *refs):
    lefts, rights, outs, total = refs[:4], refs[4:12], refs[12:16], refs[16]
    mine = where[0]
    half = mine // 4
    value = jnp.zeros((576, 512), F32)
    for n, left in enumerate(lefts):
        source = half if n < 2 else 1 - half
        rows = [right[source] for right in rights[n % 2 * 4 : n % 2 * 4 + 4]]
        value = value + nn(left[...], jnp.concatenate(rows, axis=0))
    total[...] = (value * (1.0 / math.sqrt(32768.0))).astype(BF)
    for k, out in enumerate(outs):
        out[...] = total[:, pl.ds(pl.multiple_of((mine % 4 ^ k) * HEAD, HEAD), HEAD)]


def merge_kernel(where, *refs):
    mine = where[0]
    for k, piece in enumerate(refs[:4]):
        refs[4][mine % 4 ^ k] = piece[1 - mine // 4]


def sum_kernel(where, *refs):
    total = refs[8]
    z_hi = where[2]
    value = refs[0][...].astype(F32)
    for ref in refs[1:4]:
        value = value + ref[...].astype(F32)
    total[...] = value.astype(BF)
    for k, out in enumerate(refs[4:8]):
        out[...] = total[pl.ds(pl.multiple_of((z_hi ^ k) * 144, 16), 144)]


def last_kernel(*refs):
    total = refs[0][...].astype(F32)
    for ref in refs[1:4]:
        total = total + ref[...].astype(F32)
    refs[4][...] = total


def unpack_kernel(where, *refs):
    pieces = refs[:4]
    crossed, near, far, query_grad, key_grad, value_grad = refs[4:]
    mine = where[0]
    half = mine // 4
    for k, piece in enumerate(pieces):
        head = mine ^ k
        wide = pl.ds(pl.multiple_of(head * 256, 256), 256)
        thin = pl.ds(pl.multiple_of(head * 128, 128), 128)
        query_grad[:, wide] = piece[half, :, 0:256]
        key_grad[:, thin] = piece[half, :, 256:384]
        head = (1 - half) * 4 + k
        wide = pl.ds(pl.multiple_of(head * 256, 256), 256)
        thin = pl.ds(pl.multiple_of(head * 128, 128), 128)
        query_grad[:, wide] = crossed[k, :, 0:256]
        key_grad[:, thin] = crossed[k, :, 256:384]
    value_grad[:, pl.ds(pl.multiple_of(half * 512, 512), 512)] = near[...]
    value_grad[:, pl.ds(pl.multiple_of((1 - half) * 512, 512), 512)] = far[...]


SMEM = pl.BlockSpec(memory_space=pltpu.SMEM)
VMEM = pl.BlockSpec(memory_space=pltpu.VMEM)
ANY = pl.BlockSpec(memory_space=pl.ANY)


def shape(*dims, dtype=BF):
    return jax.ShapeDtypeStruct(dims, dtype)


def call(kernel, outs, ins, scratch=(), flops=0, moved=0, limit=16, place=VMEM):
    return pl.pallas_call(
        kernel,
        out_shape=outs,
        in_specs=ins,
        out_specs=jax.tree.map(lambda _: place, outs),
        scratch_shapes=list(scratch),
        compiler_params=pltpu.CompilerParams(vmem_limit_bytes=limit * MIB),
        cost_estimate=pl.CostEstimate(flops=flops, bytes_accessed=moved, transcendentals=0),
    )


def body(
    queries, key_states, value_states, saved_output, output_grad, layer_input, document_lengths
):
    mine = lax.axis_index("ctx")
    dp = lax.axis_index("dp")
    x = dp // 8
    packed = call(
        pack_kernel,
        shape(BLOCKS, ROWS + TAIL, PACKED),
        [ANY] * 5,
        [
            pltpu.VMEM((ROWS, 2048), BF),
            pltpu.VMEM((ROWS, 1024), BF),
            pltpu.VMEM((ROWS, 1024), BF),
            pltpu.VMEM((ROWS, 2048), BF),
            pltpu.VMEM((ROWS, 2048), BF),
            pltpu.SemaphoreType.DMA((5,)),
        ],
        limit=60,
    )(queries[0], key_states[0], value_states[0], output_grad[0], saved_output[0])
    where = after(jnp.stack([mine, dp % 2, dp // 2 % 4]).astype(jnp.int32), packed)
    arrived = lax.all_to_all(packed, "ctx", 0, 0, tiled=True)

    inputs = layer_input[0]
    own = []
    for k in range(4):
        piece = lax.dynamic_slice(inputs, (0, (x ^ k) * 1152), (ROWS, 1152))
        own.append(over_x(after(piece, packed), k))
    near_rows, far_rows = call(
        turn_kernel,
        [shape(576, 512)] * 2,
        [SMEM] + [VMEM] * 4,
        [pltpu.VMEM((1152, ROWS), BF)],
    )(where, *own)
    far_rows = over_core(far_rows)
    across_near = over_ctx(near_rows, 4)

    results = call(
        attention_kernel,
        [shape(2, ROWS, BACK)] * 4 + [shape(2, ROWS, HEAD)] * 4,
        [SMEM, SMEM, VMEM],
        [
            pltpu.VMEM((BLOCKS, HEAD, ROWS), BF),
            pltpu.VMEM((BLOCKS, ROWS, 256), BF),
            pltpu.VMEM((BLOCKS, ROWS, HEAD), F32),
            pltpu.VMEM((BLOCKS, ROWS, HEAD), F32),
        ],
        flops=4_000_000_000,
        moved=4_000_000,
    )(where, document_lengths, arrived)
    backs, values = results[:4], results[4:]

    across_far = over_ctx(after(far_rows, values[0]), 4)
    early = over_y(backs[1], 1)
    pieces = [after(over_y(values[k], k), across_near, early) for k in range(4)]
    joined, near, far = call(
        join_kernel,
        [shape(2, ROWS, 512), shape(ROWS, 512), shape(ROWS, 512)],
        [SMEM] + [VMEM] * 4,
    )(where, *pieces)
    rights = [over_x(joined, k) for k in range(4)]
    rights = rights + [over_core(right) for right in rights]
    returned = [early if k == 1 else over_y(after(backs[k], joined), k) for k in range(4)]

    parts = call(
        weight_kernel,
        [shape(576, HEAD)] * 4,
        [SMEM] + [VMEM] * 12,
        [pltpu.VMEM((576, 512), BF)],
        flops=1_300_000_000,
        moved=4_000_000,
    )(where, after(near_rows, *returned), far_rows, across_near, across_far, *rights)
    crossed = call(merge_kernel, shape(4, ROWS, BACK), [SMEM] + [VMEM] * 4)(
        where, *[after(piece, parts[0]) for piece in returned]
    )
    crossed = over_ctx(crossed, 4)
    far = over_ctx(far, 4)
    reduced = [over_y(parts[k], k) for k in range(4)]
    blocks = call(
        sum_kernel, [shape(144, HEAD)] * 4, [SMEM] + [VMEM] * 4, [pltpu.VMEM((576, HEAD), BF)]
    )(where, *reduced)
    landed = [over_z(blocks[k], k) for k in range(4)]
    query_grad, key_grad, value_grad = call(
        unpack_kernel,
        [shape(ROWS, 2048), shape(ROWS, 1024), shape(ROWS, 1024)],
        [SMEM] + [VMEM] * 7,
    )(where, *returned, crossed, near, far)
    landed[1] = after(landed[1], query_grad)
    weight_grad = call(last_kernel, shape(144, HEAD, dtype=F32), [VMEM] * 4)(*landed)
    return query_grad[None], key_grad[None], value_grad[None], weight_grad


def solution(mesh):
    return jax.shard_map(
        body,
        mesh=mesh,
        in_specs=(P("dp", "ctx", None),) * 6 + (P("dp", None),),
        out_specs=(P("dp", "ctx", None),) * 3 + (P("dp", "ctx"),),
        check_vma=False,
    )
```

```python
import math

import jax
import jax.numpy as jnp
from jax import lax
from jax.experimental import pallas as pl
from jax.experimental.pallas import tpu as pltpu
from jax.sharding import PartitionSpec as P

ROWS = 128
HEAD = 128
BLOCKS = 8
TAIL = 16
PAIR = 256
PACKED = 768
BACK = 384
CAP = 50.0
SCALE = 144.0 ** (-0.5)
BF = jnp.bfloat16
F32 = jnp.float32
MIB = 1024 * 1024


def spread(block, place):
    route = []
    for ctx in range(8):
        for dp in range(32):
            here = (dp // 8, ctx % 4, (dp // 2) % 4 * 2 + ctx // 4, dp % 2)
            x, y, z, core = place(*here)
            x, y, z = x % 4, y % 4, z % 8
            route.append((ctx * 32 + dp, ((z % 2) * 4 + y) * 32 + x * 8 + z // 2 * 2 + core))
    return lax.ppermute(block, ("ctx", "dp"), route)


def over_ctx(block, k):
    return spread(block, lambda x, y, z, c: (x, y ^ k % 4, z ^ k // 4, c)) if k else block


def over_x(block, k):
    return spread(block, lambda x, y, z, c: (x ^ k, y, z, c)) if k else block


def over_y(block, k):
    return over_ctx(block, k)


def over_z(block, k):
    return spread(block, lambda x, y, z, c: (x, y, z ^ 2 * k, c)) if k else block


def over_core(block):
    return spread(block, lambda x, y, z, c: (x, y, z, 1 - c))


def after(value, *others):
    return lax.optimization_barrier((value, *others))[0]


def nt(left, right):
    return lax.dot_general(left, right, (((1,), (1,)), ((), ())), preferred_element_type=F32)


def nn(left, right):
    return lax.dot_general(left, right, (((1,), (0,)), ((), ())), preferred_element_type=F32)


def split_three(value):
    first = value.astype(BF)
    rest = value - first.astype(F32)
    second = rest.astype(BF)
    third = (rest - second.astype(F32)).astype(BF)
    return first, second, third


def pack_kernel(*refs):
    out = refs[5]
    q, k, v, do, o = refs[6:11]
    sems = refs[11]
    copies = []
    for n, (source, held) in enumerate(zip(refs[:5], refs[6:11])):
        copy = pltpu.make_async_copy(source, held, sems.at[n])
        copy.start()
        copies.append(copy)
    for copy in copies:
        copy.wait()
    product = do[...].astype(F32) * o[...].astype(F32)
    high = product.astype(BF)
    low = (product - high.astype(F32)).astype(BF)
    row = lax.broadcasted_iota(jnp.int32, (TAIL, 2048), 0)
    col = lax.broadcasted_iota(jnp.int32, (TAIL, 2048), 1)
    pick = (row == col // HEAD).astype(BF)
    delta = nt(pick, high) + nt(pick, low)
    first, second, third = split_three(delta)
    for n in range(BLOCKS):
        out[n, 0:ROWS, 0:256] = q[:, n * 256 : (n + 1) * 256]
        out[n, 0:ROWS, 256:512] = do[:, n * 256 : (n + 1) * 256]
        out[n, 0:ROWS, 512:640] = k[:, n * 128 : (n + 1) * 128]
        out[n, 0:ROWS, 640:768] = v[:, n * 128 : (n + 1) * 128]
        out[n, ROWS:, 0:128] = first
        out[n, ROWS:, 128:256] = second
        out[n, ROWS:, 256:384] = third
        out[n, ROWS:, 384:768] = jnp.zeros((TAIL, 384), BF)


def attention_kernel(where, lengths, *refs):
    held = refs[0]
    backs = refs[1:5]
    values = refs[5:7]
    key_turned, dq, dk, dv = refs[7:]
    mine = where[0]
    dk[...] = jnp.zeros_like(dk)
    dv[...] = jnp.zeros_like(dv)
    ends = []
    total = 0
    for d in range(8):
        total = total + lengths[0, d]
        ends.append(total)
    for n in range(BLOCKS):
        key_turned[n] = held[n, 0:ROWS, 512:640].T

    def block(b, carry):
        base = b * PAIR
        first = 0
        for end in ends:
            first = jnp.where(base >= end, end, first)
        kb0 = first // ROWS
        count = 2 * b + 2 - kb0
        lane = lax.broadcasted_iota(jnp.int32, (1, 2 * PAIR), 1)
        query = base + lane % PAIR
        begin = jnp.zeros((1, 2 * PAIR), jnp.int32)
        for end in ends:
            begin = jnp.where(query >= end, end, begin)
        head = lax.broadcasted_iota(jnp.int32, (TAIL, ROWS), 0)
        tails = []
        for n in range(2):
            tail = held[2 * b + n, ROWS:, 0:384].astype(F32)
            tails.append(tail[:, 0:128] + tail[:, 128:256] + tail[:, 256:384])
        delta = jnp.concatenate(
            [
                jnp.sum(jnp.where(head == 2 * mine + s, tail, 0.0), axis=0, keepdims=True)
                for s in range(2)
                for tail in tails
            ],
            axis=1,
        )

        def stacked(at):
            return jnp.concatenate(
                [
                    held[2 * b + n, 0:ROWS, at + s * 128 : at + s * 128 + 128]
                    for s in range(2)
                    for n in range(2)
                ],
                axis=0,
            )

        queries, grads = stacked(0), stacked(256)
        sub = lax.broadcasted_iota(jnp.int32, (ROWS, 2 * PAIR), 0)

        def window(number):
            powers, tanhs = [], []
            sums = jnp.zeros((1, 2 * PAIR), F32)
            for n in range(number):
                kb = kb0 + n
                raw = nt(held[kb, 0:ROWS, 512:640], queries)
                tanh = jnp.tanh(raw * (SCALE / CAP))
                key = sub + kb * ROWS
                live = key >= begin
                if n >= number - 2:
                    live = live & (key <= query)
                power = jnp.where(live, jnp.exp(CAP * tanh), 0.0)
                sums = sums + jnp.sum(power, axis=0, keepdims=True)
                powers.append(power)
                tanhs.append(tanh)
            inverse = 1.0 / sums
            turned = jnp.zeros((HEAD, 2 * PAIR), F32)
            for n in range(number):
                kb = kb0 + n
                prob = powers[n] * inverse
                dprob = nt(held[kb, 0:ROWS, 640:768], grads)
                slope = SCALE - (SCALE * tanhs[n]) * tanhs[n]
                dscore = (prob * (dprob - delta) * slope).astype(BF)
                dv[kb] += nn(prob.astype(BF), grads)
                dk[kb] += nn(dscore, queries)
                turned = turned + nn(key_turned[kb], dscore)
            straight = turned.T.astype(BF)
            for s in range(2):
                for n in range(2):
                    at = (s * 2 + n) * ROWS
                    dq[2 * b + n, :, s * 128 : s * 128 + 128] = straight[at : at + ROWS]

        for number in range(2, 7):

            @pl.when(count == number)
            def _():
                window(number)

        return carry

    lax.fori_loop(0, BLOCKS // 2, block, 0)
    for k in range(4):
        for half in range(2):
            block = half * 4 + (mine % 4 ^ k)
            at = k % 2 * HEAD
            backs[k][half, :, at : at + 256] = dq[block]
            backs[k][half, :, at + 256 : at + 384] = dk[block].astype(BF)
            value = backs[k] if k % 2 else values[k // 2]
            value[half, :, 0:HEAD] = dv[block].astype(BF)


def turn_kernel(where, *refs):
    pieces, near, far, turned = refs[:4], refs[4], refs[5], refs[6]
    core = where[1]
    for n in range(4):
        turned[...] = pieces[n][...].T
        lanes = slice(n * ROWS, (n + 1) * ROWS)
        for z in range(4):
            rows = pl.ds(z * 144, 144)
            near[rows, lanes] = turned[pl.ds(pl.multiple_of((z * 2 + core) * 144, 16), 144)]
            far[rows, lanes] = turned[pl.ds(pl.multiple_of((z * 2 + 1 - core) * 144, 16), 144)]


def join_kernel(where, *refs):
    pieces, joined, near, far = refs[:4], refs[4], refs[5], refs[6]
    mine = where[0]
    half = mine // 4
    for k, piece in enumerate(pieces):
        columns = pl.ds(pl.multiple_of((mine % 4 ^ k) * HEAD, HEAD), HEAD)
        joined[0, :, columns] = piece[0, :, 0:HEAD]
        joined[1, :, columns] = piece[1, :, 0:HEAD]
    near[...] = joined[half]
    far[...] = joined[1 - half]


def weight_kernel(where, *refs):
    lefts, rights, outs, total = refs[:4], refs[4:12], refs[12:16], refs[16]
    mine = where[0]
    half = mine // 4
    value = jnp.zeros((576, 512), F32)
    for n, left in enumerate(lefts):
        source = half if n < 2 else 1 - half
        rows = [right[source] for right in rights[n % 2 * 4 : n % 2 * 4 + 4]]
        value = value + nn(left[...], jnp.concatenate(rows, axis=0))
    total[...] = (value * (1.0 / math.sqrt(32768.0))).astype(BF)
    for k, out in enumerate(outs):
        out[...] = total[:, pl.ds(pl.multiple_of((mine % 4 ^ k) * HEAD, HEAD), HEAD)]


def merge_kernel(where, *refs):
    mine = where[0]
    for k, piece in enumerate(refs[:4]):
        at = k % 2 * HEAD
        refs[4][mine % 4 ^ k] = piece[1 - mine // 4, :, at : at + BACK]


def sum_kernel(where, *refs):
    keep, send, total = refs[4:7]
    z_hi = where[2]
    value = refs[0][...].astype(F32)
    for ref in refs[1:4]:
        value = value + ref[...].astype(F32)
    total[...] = value.astype(BF)
    for out, order in ((keep, (0, 3)), (send, (1, 2))):
        for n, k in enumerate(order):
            out[n] = total[pl.ds(pl.multiple_of((z_hi ^ k) * 144, 16), 144)]


def fold_kernel(keep, landed, own, other):
    own[...] = keep[0].astype(F32) + landed[0].astype(F32)
    other[...] = (keep[1].astype(F32) + landed[1].astype(F32)).astype(BF)


def last_kernel(own, landed, out):
    out[...] = own[...] + landed[...].astype(F32)


def unpack_kernel(where, *refs):
    pieces = refs[:4]
    crossed, near, far, query_grad, key_grad, value_grad = refs[4:]
    mine = where[0]
    half = mine // 4
    for k, piece in enumerate(pieces):
        head = mine ^ k
        wide = pl.ds(pl.multiple_of(head * 256, 256), 256)
        thin = pl.ds(pl.multiple_of(head * 128, 128), 128)
        at = k % 2 * HEAD
        query_grad[:, wide] = piece[half, :, at : at + 256]
        key_grad[:, thin] = piece[half, :, at + 256 : at + 384]
        head = (1 - half) * 4 + k
        wide = pl.ds(pl.multiple_of(head * 256, 256), 256)
        thin = pl.ds(pl.multiple_of(head * 128, 128), 128)
        query_grad[:, wide] = crossed[k, :, 0:256]
        key_grad[:, thin] = crossed[k, :, 256:384]
    value_grad[:, pl.ds(pl.multiple_of(half * 512, 512), 512)] = near[...]
    value_grad[:, pl.ds(pl.multiple_of((1 - half) * 512, 512), 512)] = far[...]


SMEM = pl.BlockSpec(memory_space=pltpu.SMEM)
VMEM = pl.BlockSpec(memory_space=pltpu.VMEM)
ANY = pl.BlockSpec(memory_space=pl.ANY)


def shape(*dims, dtype=BF):
    return jax.ShapeDtypeStruct(dims, dtype)


def call(kernel, outs, ins, scratch=(), flops=0, moved=0, limit=16, place=VMEM):
    return pl.pallas_call(
        kernel,
        out_shape=outs,
        in_specs=ins,
        out_specs=jax.tree.map(lambda _: place, outs),
        scratch_shapes=list(scratch),
        compiler_params=pltpu.CompilerParams(vmem_limit_bytes=limit * MIB),
        cost_estimate=pl.CostEstimate(flops=flops, bytes_accessed=moved, transcendentals=0),
    )


def body(
    queries, key_states, value_states, saved_output, output_grad, layer_input, document_lengths
):
    mine = lax.axis_index("ctx")
    dp = lax.axis_index("dp")
    x = dp // 8
    packed = call(
        pack_kernel,
        shape(BLOCKS, ROWS + TAIL, PACKED),
        [ANY] * 5,
        [
            pltpu.VMEM((ROWS, 2048), BF),
            pltpu.VMEM((ROWS, 1024), BF),
            pltpu.VMEM((ROWS, 1024), BF),
            pltpu.VMEM((ROWS, 2048), BF),
            pltpu.VMEM((ROWS, 2048), BF),
            pltpu.SemaphoreType.DMA((5,)),
        ],
        limit=60,
    )(queries[0], key_states[0], value_states[0], output_grad[0], saved_output[0])
    where = after(jnp.stack([mine, dp % 2, dp // 2 % 4]).astype(jnp.int32), packed)
    arrived = lax.all_to_all(packed, "ctx", 0, 0, tiled=True)

    inputs = layer_input[0]
    own = []
    for k in range(4):
        piece = lax.dynamic_slice(inputs, (0, (x ^ k) * 1152), (ROWS, 1152))
        own.append(over_x(after(piece, packed), k))
    near_rows, far_rows = call(
        turn_kernel,
        [shape(576, 512)] * 2,
        [SMEM] + [VMEM] * 4,
        [pltpu.VMEM((1152, ROWS), BF)],
    )(where, *own)
    far_rows = over_core(far_rows)
    across_near = over_ctx(near_rows, 4)

    results = call(
        attention_kernel,
        [shape(2, ROWS, BACK), shape(2, ROWS, 512)] * 2 + [shape(2, ROWS, HEAD)] * 2,
        [SMEM, SMEM, VMEM],
        [
            pltpu.VMEM((BLOCKS, HEAD, ROWS), BF),
            pltpu.VMEM((BLOCKS, ROWS, 256), BF),
            pltpu.VMEM((BLOCKS, ROWS, HEAD), F32),
            pltpu.VMEM((BLOCKS, ROWS, HEAD), F32),
        ],
        flops=4_000_000_000,
        moved=4_000_000,
    )(where, document_lengths, arrived)
    backs, values = results[:4], results[4:]

    across_far = over_ctx(after(far_rows, values[0]), 4)
    first, third = over_y(backs[1], 1), over_y(backs[3], 3)
    pieces = [values[0], first, over_y(values[1], 2), third]
    joined, near, far = call(
        join_kernel,
        [shape(2, ROWS, 512), shape(ROWS, 512), shape(ROWS, 512)],
        [SMEM] + [VMEM] * 4,
    )(where, *pieces)
    rights = [over_x(joined, k) for k in range(4)]
    rights = rights + [over_core(right) for right in rights]
    second = over_y(after(backs[2], joined), 2)
    returned = [backs[0], first, second, third]

    parts = call(
        weight_kernel,
        [shape(576, HEAD)] * 4,
        [SMEM] + [VMEM] * 12,
        [pltpu.VMEM((576, 512), BF)],
        flops=1_300_000_000,
        moved=4_000_000,
    )(where, after(near_rows, second), far_rows, across_near, across_far, *rights)
    crossed = call(merge_kernel, shape(4, ROWS, BACK), [SMEM] + [VMEM] * 4)(
        where, *[after(piece, parts[0]) for piece in returned]
    )
    crossed = over_ctx(crossed, 4)
    far = over_ctx(far, 4)
    reduced = [over_y(parts[k], k) for k in range(4)]
    keep, send = call(
        sum_kernel, [shape(2, 144, HEAD)] * 2, [SMEM] + [VMEM] * 4, [pltpu.VMEM((576, HEAD), BF)]
    )(where, *reduced)
    own, other = call(
        fold_kernel, [shape(144, HEAD, dtype=F32), shape(144, HEAD)], [VMEM] * 2
    )(keep, over_z(send, 1))
    landed = over_z(other, 3)
    query_grad, key_grad, value_grad = call(
        unpack_kernel,
        [shape(ROWS, 2048), shape(ROWS, 1024), shape(ROWS, 1024)],
        [SMEM] + [VMEM] * 7,
    )(where, *returned, crossed, near, far)
    own = after(own, query_grad)
    weight_grad = call(last_kernel, shape(144, HEAD, dtype=F32), [VMEM] * 2)(own, landed)
    return query_grad[None], key_grad[None], value_grad[None], weight_grad


def solution(mesh):
    return jax.shard_map(
        body,
        mesh=mesh,
        in_specs=(P("dp", "ctx", None),) * 6 + (P("dp", None),),
        out_specs=(P("dp", "ctx", None),) * 3 + (P("dp", "ctx"),),
        check_vma=False,
    )
```

```python
import math

import jax
import jax.numpy as jnp
from jax import lax
from jax.experimental import pallas as pl
from jax.experimental.pallas import tpu as pltpu
from jax.sharding import PartitionSpec as P

ROWS = 128
HEAD = 128
BLOCKS = 8
TAIL = 16
PAIR = 256
PACKED = 768
BACK = 384
CAP = 50.0
SCALE = 144.0 ** (-0.5)
BF = jnp.bfloat16
F32 = jnp.float32
MIB = 1024 * 1024


def spread(block, place):
    route = []
    for ctx in range(8):
        for dp in range(32):
            here = (dp // 8, ctx % 4, (dp // 2) % 4 * 2 + ctx // 4, dp % 2)
            x, y, z, core = place(*here)
            x, y, z = x % 4, y % 4, z % 8
            route.append((ctx * 32 + dp, ((z % 2) * 4 + y) * 32 + x * 8 + z // 2 * 2 + core))
    return lax.ppermute(block, ("ctx", "dp"), route)


def over_ctx(block, k):
    return spread(block, lambda x, y, z, c: (x, y ^ k % 4, z ^ k // 4, c)) if k else block


def over_x(block, k):
    return spread(block, lambda x, y, z, c: (x ^ k, y, z, c)) if k else block


def over_y(block, k):
    return over_ctx(block, k)


def over_z(block, k):
    return spread(block, lambda x, y, z, c: (x, y, z ^ 2 * k, c)) if k else block


def over_core(block):
    return spread(block, lambda x, y, z, c: (x, y, z, 1 - c))


def after(value, *others):
    return lax.optimization_barrier((value, *others))[0]


def nt(left, right):
    return lax.dot_general(left, right, (((1,), (1,)), ((), ())), preferred_element_type=F32)


def nn(left, right):
    return lax.dot_general(left, right, (((1,), (0,)), ((), ())), preferred_element_type=F32)


def split_three(value):
    first = value.astype(BF)
    rest = value - first.astype(F32)
    second = rest.astype(BF)
    third = (rest - second.astype(F32)).astype(BF)
    return first, second, third


def pack_kernel(*refs):
    out = refs[5]
    q, k, v, do, o = refs[6:11]
    sems = refs[11]
    copies = []
    for n, (source, held) in enumerate(zip(refs[:5], refs[6:11])):
        copy = pltpu.make_async_copy(source, held, sems.at[n])
        copy.start()
        copies.append(copy)
    for copy in copies:
        copy.wait()
    product = do[...].astype(F32) * o[...].astype(F32)
    high = product.astype(BF)
    low = (product - high.astype(F32)).astype(BF)
    row = lax.broadcasted_iota(jnp.int32, (TAIL, 2048), 0)
    col = lax.broadcasted_iota(jnp.int32, (TAIL, 2048), 1)
    pick = (row == col // HEAD).astype(BF)
    delta = nt(pick, high) + nt(pick, low)
    first, second, third = split_three(delta)
    for n in range(BLOCKS):
        out[n, 0:ROWS, 0:256] = q[:, n * 256 : (n + 1) * 256]
        out[n, 0:ROWS, 256:512] = do[:, n * 256 : (n + 1) * 256]
        out[n, 0:ROWS, 512:640] = k[:, n * 128 : (n + 1) * 128]
        out[n, 0:ROWS, 640:768] = v[:, n * 128 : (n + 1) * 128]
        out[n, ROWS:, 0:128] = first
        out[n, ROWS:, 128:256] = second
        out[n, ROWS:, 256:384] = third
        out[n, ROWS:, 384:768] = jnp.zeros((TAIL, 384), BF)


def attention_kernel(where, lengths, *refs):
    held = refs[0]
    backs = refs[1:5]
    values = refs[5:7]
    key_turned, dq, dk, dv = refs[7:]
    mine = where[0]
    dk[...] = jnp.zeros_like(dk)
    dv[...] = jnp.zeros_like(dv)
    ends = []
    total = 0
    for d in range(8):
        total = total + lengths[0, d]
        ends.append(total)
    for n in range(BLOCKS):
        key_turned[n] = held[n, 0:ROWS, 512:640].T

    def block(b, carry):
        base = b * PAIR
        first = 0
        for end in ends:
            first = jnp.where(base >= end, end, first)
        kb0 = first // ROWS
        count = 2 * b + 2 - kb0
        lane = lax.broadcasted_iota(jnp.int32, (1, 2 * PAIR), 1)
        query = base + lane % PAIR
        begin = jnp.zeros((1, 2 * PAIR), jnp.int32)
        for end in ends:
            begin = jnp.where(query >= end, end, begin)
        head = lax.broadcasted_iota(jnp.int32, (TAIL, ROWS), 0)
        tails = []
        for n in range(2):
            tail = held[2 * b + n, ROWS:, 0:384].astype(F32)
            tails.append(tail[:, 0:128] + tail[:, 128:256] + tail[:, 256:384])
        delta = jnp.concatenate(
            [
                jnp.sum(jnp.where(head == 2 * mine + s, tail, 0.0), axis=0, keepdims=True)
                for s in range(2)
                for tail in tails
            ],
            axis=1,
        )

        def stacked(at):
            return jnp.concatenate(
                [
                    held[2 * b + n, 0:ROWS, at + s * 128 : at + s * 128 + 128]
                    for s in range(2)
                    for n in range(2)
                ],
                axis=0,
            )

        queries, grads = stacked(0), stacked(256)
        sub = lax.broadcasted_iota(jnp.int32, (ROWS, 2 * PAIR), 0)

        def window(number):
            powers, tanhs = [], []
            sums = jnp.zeros((1, 2 * PAIR), F32)
            for n in range(number):
                kb = kb0 + n
                raw = nt(held[kb, 0:ROWS, 512:640], queries)
                tanh = jnp.tanh(raw * (SCALE / CAP))
                key = sub + kb * ROWS
                live = key >= begin
                if n >= number - 2:
                    live = live & (key <= query)
                power = jnp.where(live, jnp.exp(CAP * tanh), 0.0)
                sums = sums + jnp.sum(power, axis=0, keepdims=True)
                powers.append(power)
                tanhs.append(tanh)
            inverse = 1.0 / sums
            turned = jnp.zeros((HEAD, 2 * PAIR), F32)
            for n in range(number):
                kb = kb0 + n
                prob = powers[n] * inverse
                dprob = nt(held[kb, 0:ROWS, 640:768], grads)
                slope = SCALE - (SCALE * tanhs[n]) * tanhs[n]
                dscore = (prob * (dprob - delta) * slope).astype(BF)
                dv[kb] += nn(prob.astype(BF), grads)
                dk[kb] += nn(dscore, queries)
                turned = turned + nn(key_turned[kb], dscore)
            straight = turned.T.astype(BF)
            for s in range(2):
                for n in range(2):
                    at = (s * 2 + n) * ROWS
                    dq[2 * b + n, :, s * 128 : s * 128 + 128] = straight[at : at + ROWS]

        for number in range(2, 7):

            @pl.when(count == number)
            def _():
                window(number)

        return carry

    lax.fori_loop(0, BLOCKS // 2, block, 0)
    for k in range(4):
        for half in range(2):
            block = half * 4 + (mine % 4 ^ k)
            at = k % 2 * HEAD
            backs[k][half, :, at : at + 256] = dq[block]
            backs[k][half, :, at + 256 : at + 384] = dk[block].astype(BF)
            value = backs[k] if k % 2 else values[k // 2]
            value[half, :, 0:HEAD] = dv[block].astype(BF)


def turn_kernel(where, *refs):
    pieces, near, far, turned = refs[:4], refs[4], refs[5], refs[6]
    core = where[1]
    for n in range(4):
        turned[...] = pieces[n][...].T
        lanes = slice(n * ROWS, (n + 1) * ROWS)
        for z in range(4):
            rows = pl.ds(z * 144, 144)
            near[rows, lanes] = turned[pl.ds(pl.multiple_of((z * 2 + core) * 144, 16), 144)]
            far[rows, lanes] = turned[pl.ds(pl.multiple_of((z * 2 + 1 - core) * 144, 16), 144)]


def join_kernel(where, *refs):
    pieces, joined, near, far = refs[:4], refs[4], refs[5], refs[6]
    mine = where[0]
    half = mine // 4
    for k, piece in enumerate(pieces):
        columns = pl.ds(pl.multiple_of((mine % 4 ^ k) * HEAD, HEAD), HEAD)
        joined[0, :, columns] = piece[0, :, 0:HEAD]
        joined[1, :, columns] = piece[1, :, 0:HEAD]
    near[...] = joined[half]
    far[...] = joined[1 - half]


def weight_kernel(where, *refs):
    lefts, rights, outs, total = refs[:4], refs[4:12], refs[12:16], refs[16]
    mine = where[0]
    half = mine // 4
    value = jnp.zeros((576, 512), F32)
    for n, left in enumerate(lefts):
        source = half if n < 2 else 1 - half
        rows = [right[source] for right in rights[n % 2 * 4 : n % 2 * 4 + 4]]
        value = value + nn(left[...], jnp.concatenate(rows, axis=0))
    total[...] = (value * (1.0 / math.sqrt(32768.0))).astype(BF)
    for k, out in enumerate(outs):
        out[...] = total[:, pl.ds(pl.multiple_of((mine % 4 ^ k) * HEAD, HEAD), HEAD)]


def merge_kernel(where, *refs):
    mine = where[0]
    for k, piece in enumerate(refs[:4]):
        at = k % 2 * HEAD
        refs[4][mine % 4 ^ k] = piece[1 - mine // 4, :, at : at + BACK]


def sum_kernel(where, *refs):
    keep, send, total = refs[4:7]
    z_hi = where[2]
    value = refs[0][...].astype(F32)
    for ref in refs[1:4]:
        value = value + ref[...].astype(F32)
    total[...] = value.astype(BF)
    for out, order in ((keep, (0, 3)), (send, (1, 2))):
        for n, k in enumerate(order):
            out[n] = total[pl.ds(pl.multiple_of((z_hi ^ k) * 144, 16), 144)]


def fold_kernel(keep, landed, own, other):
    own[...] = keep[0].astype(F32) + landed[0].astype(F32)
    other[...] = (keep[1].astype(F32) + landed[1].astype(F32)).astype(BF)


def last_kernel(own, landed, out):
    out[...] = own[...] + landed[...].astype(F32)


def unpack_kernel(where, *refs):
    pieces = refs[:4]
    crossed, near, far, query_grad, key_grad, value_grad = refs[4:]
    mine = where[0]
    half = mine // 4
    for k, piece in enumerate(pieces):
        head = mine ^ k
        wide = pl.ds(pl.multiple_of(head * 256, 256), 256)
        thin = pl.ds(pl.multiple_of(head * 128, 128), 128)
        at = k % 2 * HEAD
        query_grad[:, wide] = piece[half, :, at : at + 256]
        key_grad[:, thin] = piece[half, :, at + 256 : at + 384]
        head = (1 - half) * 4 + k
        wide = pl.ds(pl.multiple_of(head * 256, 256), 256)
        thin = pl.ds(pl.multiple_of(head * 128, 128), 128)
        query_grad[:, wide] = crossed[k, :, 0:256]
        key_grad[:, thin] = crossed[k, :, 256:384]
    value_grad[:, pl.ds(pl.multiple_of(half * 512, 512), 512)] = near[...]
    value_grad[:, pl.ds(pl.multiple_of((1 - half) * 512, 512), 512)] = far[...]


SMEM = pl.BlockSpec(memory_space=pltpu.SMEM)
VMEM = pl.BlockSpec(memory_space=pltpu.VMEM)
ANY = pl.BlockSpec(memory_space=pl.ANY)


def shape(*dims, dtype=BF):
    return jax.ShapeDtypeStruct(dims, dtype)


def call(kernel, outs, ins, scratch=(), flops=0, moved=0, limit=16, place=VMEM):
    return pl.pallas_call(
        kernel,
        out_shape=outs,
        in_specs=ins,
        out_specs=jax.tree.map(lambda _: place, outs),
        scratch_shapes=list(scratch),
        compiler_params=pltpu.CompilerParams(vmem_limit_bytes=limit * MIB),
        cost_estimate=pl.CostEstimate(flops=flops, bytes_accessed=moved, transcendentals=0),
    )


def body(
    queries, key_states, value_states, saved_output, output_grad, layer_input, document_lengths
):
    mine = lax.axis_index("ctx")
    dp = lax.axis_index("dp")
    x = dp // 8
    packed = call(
        pack_kernel,
        shape(BLOCKS, ROWS + TAIL, PACKED),
        [ANY] * 5,
        [
            pltpu.VMEM((ROWS, 2048), BF),
            pltpu.VMEM((ROWS, 1024), BF),
            pltpu.VMEM((ROWS, 1024), BF),
            pltpu.VMEM((ROWS, 2048), BF),
            pltpu.VMEM((ROWS, 2048), BF),
            pltpu.SemaphoreType.DMA((5,)),
        ],
        limit=60,
    )(queries[0], key_states[0], value_states[0], output_grad[0], saved_output[0])
    where = after(jnp.stack([mine, dp % 2, dp // 2 % 4]).astype(jnp.int32), packed)
    arrived = lax.all_to_all(packed, "ctx", 0, 0, tiled=True)

    inputs = layer_input[0]
    own = []
    for k in range(4):
        piece = lax.dynamic_slice(inputs, (0, (x ^ k) * 1152), (ROWS, 1152))
        own.append(over_x(after(piece, packed), k))
    near_rows, far_rows = call(
        turn_kernel,
        [shape(576, 512)] * 2,
        [SMEM] + [VMEM] * 4,
        [pltpu.VMEM((1152, ROWS), BF)],
    )(where, *own)
    across_near = over_ctx(near_rows, 4)

    results = call(
        attention_kernel,
        [shape(2, ROWS, BACK), shape(2, ROWS, 512)] * 2 + [shape(2, ROWS, HEAD)] * 2,
        [SMEM, SMEM, VMEM],
        [
            pltpu.VMEM((BLOCKS, HEAD, ROWS), BF),
            pltpu.VMEM((BLOCKS, ROWS, 256), BF),
            pltpu.VMEM((BLOCKS, ROWS, HEAD), F32),
            pltpu.VMEM((BLOCKS, ROWS, HEAD), F32),
        ],
        flops=4_000_000_000,
        moved=4_000_000,
    )(where, document_lengths, arrived)
    backs, values = results[:4], results[4:]

    far_rows = over_core(after(far_rows, values[0]))
    across_far = over_ctx(far_rows, 4)
    first, third = over_y(backs[1], 1), over_y(backs[3], 3)
    pieces = [values[0], first, over_y(values[1], 2), third]
    joined, near, far = call(
        join_kernel,
        [shape(2, ROWS, 512), shape(ROWS, 512), shape(ROWS, 512)],
        [SMEM] + [VMEM] * 4,
    )(where, *pieces)
    rights = [over_x(joined, k) for k in range(4)]
    rights = rights + [over_core(right) for right in rights]
    second = over_y(after(backs[2], joined), 2)
    returned = [backs[0], first, second, third]

    parts = call(
        weight_kernel,
        [shape(576, HEAD)] * 4,
        [SMEM] + [VMEM] * 12,
        [pltpu.VMEM((576, 512), BF)],
        flops=1_300_000_000,
        moved=4_000_000,
    )(where, after(near_rows, second), far_rows, across_near, across_far, *rights)
    crossed = call(merge_kernel, shape(4, ROWS, BACK), [SMEM] + [VMEM] * 4)(
        where, *[after(piece, parts[0]) for piece in returned]
    )
    crossed = over_ctx(crossed, 4)
    far = over_ctx(far, 4)
    reduced = [over_y(parts[k], k) for k in range(4)]
    keep, send = call(
        sum_kernel, [shape(2, 144, HEAD)] * 2, [SMEM] + [VMEM] * 4, [pltpu.VMEM((576, HEAD), BF)]
    )(where, *reduced)
    own, other = call(
        fold_kernel, [shape(144, HEAD, dtype=F32), shape(144, HEAD)], [VMEM] * 2
    )(keep, over_z(send, 1))
    landed = over_z(other, 3)
    query_grad, key_grad, value_grad = call(
        unpack_kernel,
        [shape(ROWS, 2048), shape(ROWS, 1024), shape(ROWS, 1024)],
        [SMEM] + [VMEM] * 7,
    )(where, *returned, crossed, near, far)
    own = after(own, query_grad)
    weight_grad = call(last_kernel, shape(144, HEAD, dtype=F32), [VMEM] * 2)(own, landed)
    return query_grad[None], key_grad[None], value_grad[None], weight_grad


def solution(mesh):
    return jax.shard_map(
        body,
        mesh=mesh,
        in_specs=(P("dp", "ctx", None),) * 6 + (P("dp", None),),
        out_specs=(P("dp", "ctx", None),) * 3 + (P("dp", "ctx"),),
        check_vma=False,
    )
```

```python
import math

import jax
import jax.numpy as jnp
from jax import lax
from jax.experimental import pallas as pl
from jax.experimental.pallas import tpu as pltpu
from jax.sharding import PartitionSpec as P

ROWS = 128
HEAD = 128
BLOCKS = 8
TAIL = 16
PAIR = 256
PACKED = 768
BACK = 384
CAP = 50.0
SCALE = 144.0 ** (-0.5)
BF = jnp.bfloat16
F32 = jnp.float32
MIB = 1024 * 1024


def spread(block, place):
    route = []
    for ctx in range(8):
        for dp in range(32):
            here = (dp // 8, ctx % 4, (dp // 2) % 4 * 2 + ctx // 4, dp % 2)
            x, y, z, core = place(*here)
            x, y, z = x % 4, y % 4, z % 8
            route.append((ctx * 32 + dp, ((z % 2) * 4 + y) * 32 + x * 8 + z // 2 * 2 + core))
    return lax.ppermute(block, ("ctx", "dp"), route)


def over_ctx(block, k):
    return spread(block, lambda x, y, z, c: (x, y ^ k % 4, z ^ k // 4, c)) if k else block


def over_x(block, k):
    return spread(block, lambda x, y, z, c: (x ^ k, y, z, c)) if k else block


def over_y(block, k):
    return over_ctx(block, k)


def over_z(block, k):
    return spread(block, lambda x, y, z, c: (x, y, z ^ 2 * k, c)) if k else block


def over_core(block):
    return spread(block, lambda x, y, z, c: (x, y, z, 1 - c))


def after(value, *others):
    return lax.optimization_barrier((value, *others))[0]


def nt(left, right):
    return lax.dot_general(left, right, (((1,), (1,)), ((), ())), preferred_element_type=F32)


def nn(left, right):
    return lax.dot_general(left, right, (((1,), (0,)), ((), ())), preferred_element_type=F32)


def split_three(value):
    first = value.astype(BF)
    rest = value - first.astype(F32)
    second = rest.astype(BF)
    third = (rest - second.astype(F32)).astype(BF)
    return first, second, third


def pack_kernel(*refs):
    out = refs[5]
    q, k, v, do, o = refs[6:11]
    sems = refs[11]
    copies = []
    for n, (source, held) in enumerate(zip(refs[:5], refs[6:11])):
        copy = pltpu.make_async_copy(source, held, sems.at[n])
        copy.start()
        copies.append(copy)
    for copy in copies:
        copy.wait()
    product = do[...].astype(F32) * o[...].astype(F32)
    high = product.astype(BF)
    low = (product - high.astype(F32)).astype(BF)
    row = lax.broadcasted_iota(jnp.int32, (TAIL, 2048), 0)
    col = lax.broadcasted_iota(jnp.int32, (TAIL, 2048), 1)
    pick = (row == col // HEAD).astype(BF)
    delta = nt(pick, high) + nt(pick, low)
    first, second, third = split_three(delta)
    for n in range(BLOCKS):
        out[n, 0:ROWS, 0:256] = q[:, n * 256 : (n + 1) * 256]
        out[n, 0:ROWS, 256:512] = do[:, n * 256 : (n + 1) * 256]
        out[n, 0:ROWS, 512:640] = k[:, n * 128 : (n + 1) * 128]
        out[n, 0:ROWS, 640:768] = v[:, n * 128 : (n + 1) * 128]
        out[n, ROWS:, 0:128] = first
        out[n, ROWS:, 128:256] = second
        out[n, ROWS:, 256:384] = third
        out[n, ROWS:, 384:768] = jnp.zeros((TAIL, 384), BF)


def attention_kernel(where, lengths, *refs):
    held = refs[0]
    backs = refs[1:5]
    values = refs[5:7]
    key_turned, dq, dk, dv = refs[7:]
    mine = where[0]
    dk[...] = jnp.zeros_like(dk)
    dv[...] = jnp.zeros_like(dv)
    ends = []
    total = 0
    for d in range(8):
        total = total + lengths[0, d]
        ends.append(total)
    for n in range(BLOCKS):
        key_turned[n] = held[n, 0:ROWS, 512:640].T

    def block(b, carry):
        base = b * PAIR
        first = 0
        for end in ends:
            first = jnp.where(base >= end, end, first)
        kb0 = first // ROWS
        count = 2 * b + 2 - kb0
        lane = lax.broadcasted_iota(jnp.int32, (1, 2 * PAIR), 1)
        query = base + lane % PAIR
        begin = jnp.zeros((1, 2 * PAIR), jnp.int32)
        for end in ends:
            begin = jnp.where(query >= end, end, begin)
        head = lax.broadcasted_iota(jnp.int32, (TAIL, ROWS), 0)
        tails = []
        for n in range(2):
            tail = held[2 * b + n, ROWS:, 0:384].astype(F32)
            tails.append(tail[:, 0:128] + tail[:, 128:256] + tail[:, 256:384])
        delta = jnp.concatenate(
            [
                jnp.sum(jnp.where(head == 2 * mine + s, tail, 0.0), axis=0, keepdims=True)
                for s in range(2)
                for tail in tails
            ],
            axis=1,
        )

        def stacked(at):
            return jnp.concatenate(
                [
                    held[2 * b + n, 0:ROWS, at + s * 128 : at + s * 128 + 128]
                    for s in range(2)
                    for n in range(2)
                ],
                axis=0,
            )

        queries, grads = stacked(0), stacked(256)
        sub = lax.broadcasted_iota(jnp.int32, (ROWS, 2 * PAIR), 0)

        def window(number):
            powers, tanhs = [], []
            sums = jnp.zeros((1, 2 * PAIR), F32)
            for n in range(number):
                kb = kb0 + n
                raw = nt(held[kb, 0:ROWS, 512:640], queries)
                tanh = jnp.tanh(raw * (SCALE / CAP))
                key = sub + kb * ROWS
                live = key >= begin
                if n >= number - 2:
                    live = live & (key <= query)
                power = jnp.where(live, jnp.exp(CAP * tanh), 0.0)
                sums = sums + jnp.sum(power, axis=0, keepdims=True)
                powers.append(power)
                tanhs.append(tanh)
            inverse = 1.0 / sums
            turned = jnp.zeros((HEAD, 2 * PAIR), F32)
            for n in range(number):
                kb = kb0 + n
                prob = powers[n] * inverse
                dprob = nt(held[kb, 0:ROWS, 640:768], grads)
                slope = SCALE - (SCALE * tanhs[n]) * tanhs[n]
                dscore = (prob * (dprob - delta) * slope).astype(BF)
                dv[kb] += nn(prob.astype(BF), grads)
                dk[kb] += nn(dscore, queries)
                turned = turned + nn(key_turned[kb], dscore)
            straight = turned.T.astype(BF)
            for s in range(2):
                for n in range(2):
                    at = (s * 2 + n) * ROWS
                    dq[2 * b + n, :, s * 128 : s * 128 + 128] = straight[at : at + ROWS]

        for number in range(2, 7):

            @pl.when(count == number)
            def _():
                window(number)

        return carry

    lax.fori_loop(0, BLOCKS // 2, block, 0)
    for k in range(4):
        for half in range(2):
            block = half * 4 + (mine % 4 ^ k)
            at = k % 2 * HEAD
            backs[k][half, :, at : at + 256] = dq[block]
            backs[k][half, :, at + 256 : at + 384] = dk[block].astype(BF)
            value = backs[k] if k % 2 else values[k // 2]
            value[half, :, 0:HEAD] = dv[block].astype(BF)


def turn_kernel(where, *refs):
    pieces, near, far, turned = refs[:4], refs[4], refs[5], refs[6]
    core = where[1]
    for n in range(4):
        turned[...] = pieces[n][...].T
        lanes = slice(n * ROWS, (n + 1) * ROWS)
        for z in range(4):
            rows = pl.ds(z * 144, 144)
            near[rows, lanes] = turned[pl.ds(pl.multiple_of((z * 2 + core) * 144, 16), 144)]
            far[rows, lanes] = turned[pl.ds(pl.multiple_of((z * 2 + 1 - core) * 144, 16), 144)]


def join_kernel(where, *refs):
    pieces, joined, near, far = refs[:4], refs[4], refs[5], refs[6]
    mine = where[0]
    half = mine // 4
    for k, piece in enumerate(pieces):
        columns = pl.ds(pl.multiple_of((mine % 4 ^ k) * HEAD, HEAD), HEAD)
        joined[0, :, columns] = piece[0, :, 0:HEAD]
        joined[1, :, columns] = piece[1, :, 0:HEAD]
    near[...] = joined[half]
    far[...] = joined[1 - half]


def weight_kernel(where, *refs):
    lefts, rights, outs, total = refs[:4], refs[4:12], refs[12:16], refs[16]
    mine = where[0]
    half = mine // 4
    value = jnp.zeros((576, 512), F32)
    for n, left in enumerate(lefts):
        source = half if n < 2 else 1 - half
        rows = [right[source] for right in rights[n % 2 * 4 : n % 2 * 4 + 4]]
        value = value + nn(left[...], jnp.concatenate(rows, axis=0))
    total[...] = (value * (1.0 / math.sqrt(32768.0))).astype(BF)
    for k, out in enumerate(outs):
        out[...] = total[:, pl.ds(pl.multiple_of((mine % 4 ^ k) * HEAD, HEAD), HEAD)]


def merge_kernel(where, *refs):
    mine = where[0]
    for k, piece in enumerate(refs[:4]):
        at = k % 2 * HEAD
        refs[4][mine % 4 ^ k] = piece[1 - mine // 4, :, at : at + BACK]


def sum_kernel(where, *refs):
    keep, send, total = refs[4:7]
    z_hi = where[2]
    value = refs[0][...].astype(F32)
    for ref in refs[1:4]:
        value = value + ref[...].astype(F32)
    total[...] = value.astype(BF)
    for out, order in ((keep, (0, 3)), (send, (1, 2))):
        for n, k in enumerate(order):
            out[n] = total[pl.ds(pl.multiple_of((z_hi ^ k) * 144, 16), 144)]


def fold_kernel(keep, landed, own, other):
    own[...] = keep[0].astype(F32) + landed[0].astype(F32)
    other[...] = (keep[1].astype(F32) + landed[1].astype(F32)).astype(BF)


def last_kernel(own, landed, out):
    out[...] = own[...] + landed[...].astype(F32)


def unpack_kernel(where, *refs):
    pieces = refs[:4]
    crossed, near, far, query_grad, key_grad, value_grad = refs[4:]
    mine = where[0]
    half = mine // 4
    for k, piece in enumerate(pieces):
        head = mine ^ k
        wide = pl.ds(pl.multiple_of(head * 256, 256), 256)
        thin = pl.ds(pl.multiple_of(head * 128, 128), 128)
        at = k % 2 * HEAD
        query_grad[:, wide] = piece[half, :, at : at + 256]
        key_grad[:, thin] = piece[half, :, at + 256 : at + 384]
        head = (1 - half) * 4 + k
        wide = pl.ds(pl.multiple_of(head * 256, 256), 256)
        thin = pl.ds(pl.multiple_of(head * 128, 128), 128)
        query_grad[:, wide] = crossed[k, :, 0:256]
        key_grad[:, thin] = crossed[k, :, 256:384]
    value_grad[:, pl.ds(pl.multiple_of(half * 512, 512), 512)] = near[...]
    value_grad[:, pl.ds(pl.multiple_of((1 - half) * 512, 512), 512)] = far[...]


SMEM = pl.BlockSpec(memory_space=pltpu.SMEM)
VMEM = pl.BlockSpec(memory_space=pltpu.VMEM)
ANY = pl.BlockSpec(memory_space=pl.ANY)


def shape(*dims, dtype=BF):
    return jax.ShapeDtypeStruct(dims, dtype)


def call(kernel, outs, ins, scratch=(), flops=0, moved=0, limit=16, place=VMEM):
    return pl.pallas_call(
        kernel,
        out_shape=outs,
        in_specs=ins,
        out_specs=jax.tree.map(lambda _: place, outs),
        scratch_shapes=list(scratch),
        compiler_params=pltpu.CompilerParams(vmem_limit_bytes=limit * MIB),
        cost_estimate=pl.CostEstimate(flops=flops, bytes_accessed=moved, transcendentals=0),
    )


def body(
    queries, key_states, value_states, saved_output, output_grad, layer_input, document_lengths
):
    mine = lax.axis_index("ctx")
    dp = lax.axis_index("dp")
    x = dp // 8
    packed = call(
        pack_kernel,
        shape(BLOCKS, ROWS + TAIL, PACKED),
        [ANY] * 5,
        [
            pltpu.VMEM((ROWS, 2048), BF),
            pltpu.VMEM((ROWS, 1024), BF),
            pltpu.VMEM((ROWS, 1024), BF),
            pltpu.VMEM((ROWS, 2048), BF),
            pltpu.VMEM((ROWS, 2048), BF),
            pltpu.SemaphoreType.DMA((5,)),
        ],
        limit=60,
    )(queries[0], key_states[0], value_states[0], output_grad[0], saved_output[0])
    where = after(jnp.stack([mine, dp % 2, dp // 2 % 4]).astype(jnp.int32), packed)
    arrived = lax.all_to_all(packed, "ctx", 0, 0, tiled=True)

    inputs = layer_input[0]
    own = []
    for k in range(4):
        piece = lax.dynamic_slice(inputs, (0, (x ^ k) * 1152), (ROWS, 1152))
        own.append(over_x(after(piece, packed), k))
    near_rows, far_rows = call(
        turn_kernel,
        [shape(576, 512)] * 2,
        [SMEM] + [VMEM] * 4,
        [pltpu.VMEM((1152, ROWS), BF)],
    )(where, *own)
    across_near = over_ctx(near_rows, 4)

    results = call(
        attention_kernel,
        [shape(2, ROWS, BACK), shape(2, ROWS, 512)] * 2 + [shape(2, ROWS, HEAD)] * 2,
        [SMEM, SMEM, VMEM],
        [
            pltpu.VMEM((BLOCKS, HEAD, ROWS), BF),
            pltpu.VMEM((BLOCKS, ROWS, 256), BF),
            pltpu.VMEM((BLOCKS, ROWS, HEAD), F32),
            pltpu.VMEM((BLOCKS, ROWS, HEAD), F32),
        ],
        flops=4_000_000_000,
        moved=4_000_000,
    )(where, document_lengths, arrived)
    backs, values = results[:4], results[4:]

    far_rows = over_core(after(far_rows, values[0]))
    across_far = over_ctx(far_rows, 4)
    first, third = over_y(backs[1], 1), over_y(backs[3], 3)
    pieces = [values[0], first, over_y(values[1], 2), third]
    joined, near, far = call(
        join_kernel,
        [shape(2, ROWS, 512), shape(ROWS, 512), shape(ROWS, 512)],
        [SMEM] + [VMEM] * 4,
    )(where, *pieces)
    rights = [over_x(joined, k) for k in range(4)]
    rights = rights + [over_core(right) for right in rights]
    second = over_y(after(backs[2], joined), 2)
    returned = [backs[0], first, second, third]

    crossed_blocks = call(merge_kernel, shape(4, ROWS, BACK), [SMEM] + [VMEM] * 4)(
        where, *[after(piece, rights[1]) for piece in returned]
    )
    crossed = over_ctx(crossed_blocks, 4)
    parts = call(
        weight_kernel,
        [shape(576, HEAD)] * 4,
        [SMEM] + [VMEM] * 12,
        [pltpu.VMEM((576, 512), BF)],
        flops=1_300_000_000,
        moved=4_000_000,
    )(where, after(near_rows, crossed_blocks), far_rows, across_near, across_far, *rights)
    far = over_ctx(far, 4)
    reduced = [over_y(parts[k], k) for k in range(4)]
    keep, send = call(
        sum_kernel, [shape(2, 144, HEAD)] * 2, [SMEM] + [VMEM] * 4, [pltpu.VMEM((576, HEAD), BF)]
    )(where, *reduced)
    own, other = call(
        fold_kernel, [shape(144, HEAD, dtype=F32), shape(144, HEAD)], [VMEM] * 2
    )(keep, over_z(send, 1))
    landed = over_z(other, 3)
    query_grad, key_grad, value_grad = call(
        unpack_kernel,
        [shape(ROWS, 2048), shape(ROWS, 1024), shape(ROWS, 1024)],
        [SMEM] + [VMEM] * 7,
    )(where, *returned, crossed, near, far)
    own = after(own, query_grad)
    weight_grad = call(last_kernel, shape(144, HEAD, dtype=F32), [VMEM] * 2)(own, landed)
    return query_grad[None], key_grad[None], value_grad[None], weight_grad


def solution(mesh):
    return jax.shard_map(
        body,
        mesh=mesh,
        in_specs=(P("dp", "ctx", None),) * 6 + (P("dp", None),),
        out_specs=(P("dp", "ctx", None),) * 3 + (P("dp", "ctx"),),
        check_vma=False,
    )
```
